32 devices in a mesh: band: 4 (over z), dom: 8 (over y, x, core).
Axes of the slice: x: 2, y: 2, z: 4, core: 2. Of those that a mesh axis runs over, the one named last changes fastest.
Arguments:
- orbitals: bfloat16 [32, 32, 24576], P('band', 'dom'), may hold values from -6 to 6
- occupations: int32 [32], P('band'), may hold values from 1 to 4
Outputs:
- potential: float32 [32, 24576], P('dom')
- applied: bfloat16 [32, 32, 24576], P('band', 'dom')
The draws below stay inside these ranges and needn't reach their ends.
All inputs are finite; a program needn't handle non-finite values.
Results may differ from the reference program's by a relative error of at most 0.0029.
Values sent between devices are 32-bit elements; how exact they have to be, the bound alone decides.
A program may use at most 128 MiB of HBM per device.

```python
import math
import jax
import jax.numpy as jnp
from jax import lax

NX = 128
NY = 192
LEVELS = 3
PRE = 2
POST = 2
COARSE = 48
CYCLES = 2
NZ = 32
ORBITALS = 32


def draw_orbitals(key, part):
    cells = NY * NX
    key_size = jax.random.fold_in(key, 11)
    key_sign = jax.random.fold_in(key, 12)
    key_noise = jax.random.fold_in(key, 13)
    key_gain = jax.random.fold_in(key, 14)
    key_flip = jax.random.fold_in(key, 15)
    size = jnp.exp(jax.random.uniform(key_size, (NZ, cells), jnp.float32, math.log(0.05), math.log(3.0)))
    noise = 0.5 * jax.random.normal(key_noise, (ORBITALS, NZ, cells), jnp.float32)
    sign = jnp.where(jax.random.bernoulli(key_sign, 0.5, (NZ, cells)), 1.0, -1.0).astype(jnp.float32)
    shared = sign * size
    flips = jnp.where(jax.random.bernoulli(key_flip, 0.5, (ORBITALS,)), 1.0, -1.0).astype(jnp.float32)
    gain = jax.random.uniform(key_gain, (ORBITALS,), jnp.float32, 0.7, 1.3) * flips
    values = gain[:, None, None] * shared[None] + noise
    return jnp.clip(values, -6.0, 6.0).astype(jnp.bfloat16)


def set_ends(entries, rng, least, high):
    extent = entries.shape
    place = [jax.random.randint(jax.random.fold_in(rng, axis), (), 0, extent[axis]) for axis in range(len(extent))]
    entries = entries.at[tuple(place)].set(least)
    longest = extent.index(max(extent))
    place[longest] = (place[longest] + 1) % extent[longest]
    return entries.at[tuple(place)].set(high)


def setup_inputs(seed: int = 0) -> dict:
    streams_of = jax.random.split(jax.random.key(seed), 3)
    orbitals = draw_orbitals(jax.random.fold_in(streams_of[2], 71), 0)
    occupations = set_ends(jax.random.randint(streams_of[1], (ORBITALS,), 1, 5), jax.random.fold_in(streams_of[1], 1), 1, 4).astype(jnp.int32)
    return dict(orbitals=orbitals, occupations=occupations)


screening = 0.02
relaxation = 0.8
charge_scale = 0.07


def operate(field, level):
    scale = 4.0 ** level
    padded = jnp.pad(field, 1)
    beside = padded[2:, 1:-1, 1:-1] + padded[:-2, 1:-1, 1:-1]
    beside = beside + padded[1:-1, 2:, 1:-1] + padded[1:-1, :-2, 1:-1]
    beside = beside + padded[1:-1, 1:-1, 2:] + padded[1:-1, 1:-1, :-2]
    return ((6.0 + screening * scale) * field - beside) / scale


def smooth(field, source, level, count):
    scale = 4.0 ** level
    diagonal = (6.0 + screening * scale) / scale
    for sweep in range(count):
        field = field + relaxation * (source - operate(field, level)) / diagonal
    return field


def restrict(field):
    depth, rows, cols = field.shape
    return field.reshape(depth // 2, 2, rows // 2, 2, cols // 2, 2).mean(axis=(1, 3, 5))


def prolong(field):
    return jnp.repeat(jnp.repeat(jnp.repeat(field, 2, axis=0), 2, axis=1), 2, axis=2)


def vcycle(field, source, level):
    if level == LEVELS:
        return smooth(jnp.zeros_like(source), source, level, COARSE)
    field = smooth(field, source, level, PRE)
    resid = source - operate(field, level)
    coarse = restrict(resid)
    correct = vcycle(jnp.zeros_like(coarse), coarse, level + 1)
    field = field + prolong(correct)
    return smooth(field, source, level, POST)


def reference(orbitals, occupations):
    weights = occupations.astype(jnp.float32) * 0.5

    def add_one(total, item):
        psi, weight = item
        values = psi.astype(jnp.float32)
        return total + weight * values * values, None

    start = jnp.zeros(orbitals.shape[1:], jnp.float32)
    density, unused = lax.scan(add_one, start, (orbitals, weights))
    density = density / ORBITALS
    source = charge_scale * density.reshape(NZ, NY, NX)
    field = jnp.zeros_like(source)
    for cycle in range(CYCLES):
        field = vcycle(field, source, 0)
    potential = field.reshape(NZ, NY * NX)
    applied = lax.map(lambda psi: (potential * psi.astype(jnp.float32)).astype(jnp.bfloat16), orbitals)
    return potential, applied
```

```python
import functools

import jax
import jax.numpy as jnp
import numpy as np
from jax import lax
from jax.experimental import pallas as pl
from jax.experimental.pallas import tpu as pltpu
from jax.sharding import PartitionSpec as P

NX = 128
NY = 192
COARSE = 48

screening = 0.02
relaxation = 0.8
charge_scale = 0.07

PLANES = 4
HALO = 6
OWN = HALO
WINDOW = PLANES + 2 * HALO
PAD = 8
CHUNKS = 8
LAG = 3
HALVES = 2
MOST = (4, 4, 8)
STEP = NY // CHUNKS
HALF = NY // HALVES
CENTRE = [6.0 + screening * 4.0**level for level in range(4)]
GAIN = [relaxation / centre for centre in CENTRE]
KEEP = 1.0 - relaxation


def sines(n):
    k = np.arange(1, n + 1)
    basis = np.sqrt(2.0 / (n + 1)) * np.sin(np.pi * np.outer(k, k) / (n + 1))
    return basis, 2.0 * np.cos(np.pi * k / (n + 1))


def coarse_basis(depth):
    rows, cols, copies = NY // 8, NX // 8, 8
    sz, ez = sines(depth)
    sy, ey = sines(rows)
    sx, ex = sines(cols)
    left = np.kron(sz, sy)
    into = np.zeros((NX, NX))
    into[::copies, :cols] = sx
    back = np.zeros((NX, NX))
    back[:cols] = np.repeat(sx, copies, axis=1)
    near = (ez[:, None] + ey[None, :]).reshape(-1, 1) + ex[None, :]
    rate = KEEP + GAIN[3] * near
    total = GAIN[3] * sum(rate**n for n in range(COARSE))
    weight = np.zeros((depth * rows, NX))
    weight[:, :cols] = total
    return [np.asarray(part, np.float32) for part in (left, into, back, weight)]


def kernel(
    bands, domains,
    rho, left, into, back, weight,
    out,
    acc, from_outer, from_inner, fx, va, vb, vc, hv, t0, t1, t2, t3, g,
    f1, u1a, u1b, f2, u2a, u2b, f3,
    up_s, up_r, mid_s, mid_r, down_s, down_r, near_s, near_r, far_s, far_r, hv_s, hv_r, g_s, g_r,
):
    b = lax.axis_index("band")
    d = lax.axis_index("dom")
    half = bands // 2
    lower = b < half
    inner = jnp.where(lower, b + 1, b - 1)
    outer = jnp.where(lower, b - 1, b + 1)
    has_outer = jnp.logical_and(b > 0, b < bands - 1)
    centre = jnp.logical_or(b == half - 1, b == half)
    n1, n2, n3 = 2 * domains, domains, domains // 2

    def remote(src, dst, ss, rs, dev):
        return pltpu.make_async_remote_copy(
            src_ref=src, dst_ref=dst, send_sem=ss, recv_sem=rs,
            device_id=dev, device_id_type=pl.DeviceIdType.MESH,
        )

    fx[...] = jnp.zeros_like(fx)
    barrier = pltpu.get_barrier_semaphore()

    def greet(dev):
        pl.semaphore_signal(barrier, inc=1, device_id=dev, device_id_type=pl.DeviceIdType.MESH)

    for i in range(1, domains):
        greet((b, lax.rem(d + i, domains)))
    greet((inner, d))

    @pl.when(has_outer)
    def _():
        greet((outer, d))

    for ref in (va, vb, vc, f1, u1a, u1b, f2, u2a, u2b):
        ref[...] = jnp.zeros_like(ref)

    pl.semaphore_wait(barrier, domains + jnp.where(has_outer, 1, 0))

    def part(ref, c):
        return ref.at[:, pl.ds(c * STEP, STEP), :]

    def slab(c):
        return fx.at[pl.ds(OWN, PLANES), pl.ds(PAD + c * STEP, STEP), :]

    def up(c):
        return remote(part(acc, c), part(from_outer, c), up_s.at[c], up_r.at[c], (inner, d))

    def mid(c):
        return remote(part(acc, c), part(from_inner, c), mid_s.at[c], mid_r.at[c], (inner, d))

    def down(c, dev):
        return remote(slab(c), slab(c), down_s.at[c], down_r.at[c], (dev, d))

    def near_up(c):
        rows = pl.ds(PAD + c * STEP, STEP)
        return remote(
            fx.at[pl.ds(OWN + 2, 2), rows, :], fx.at[pl.ds(OWN - 2, 2), rows, :],
            near_s.at[0, c], near_r.at[0, c], (b, d + 1),
        )

    def near_down(c):
        rows = pl.ds(PAD + c * STEP, STEP)
        return remote(
            fx.at[pl.ds(OWN, 2), rows, :], fx.at[pl.ds(OWN + 4, 2), rows, :],
            near_s.at[1, c], near_r.at[1, c], (b, d - 1),
        )

    even_d = lax.rem(d, 2) == 0
    odd_d = lax.rem(d, 2) == 1
    far = [
        (OWN, OWN - 4, 1, d < domains - 1, d > 0),
        (OWN + 2, OWN + 6, -1, d > 0, d < domains - 1),
        (OWN + 2, OWN - 6, 2, jnp.logical_and(even_d, d < domains - 2), d > 1),
        (OWN, OWN + 8, -2, jnp.logical_and(odd_d, d > 1), d < domains - 2),
    ]

    def far_copy(i, h):
        at, to, offset, _, _ = far[i]
        rows = pl.ds(PAD + h * HALF, HALF)
        return remote(
            fx.at[pl.ds(at, 2), rows, :], fx.at[pl.ds(to, 2), rows, :],
            far_s.at[i, h], far_r.at[i, h], (b, d + offset),
        )

    onward = [
        (OWN - 2, OWN - 6, 1, 2, jnp.logical_and(even_d, d > 1)),
        (OWN + 4, OWN + 8, -1, 3, jnp.logical_and(odd_d, d < domains - 2)),
    ]

    def onward_copy(i, h):
        at, to, offset, slot, _ = onward[i]
        rows = pl.ds(PAD + h * HALF, HALF)
        return remote(
            fx.at[pl.ds(at, 2), rows, :], fx.at[pl.ds(to, 2), rows, :],
            far_s.at[slot + 2, h], far_r.at[slot, h], (b, d + offset),
        )

    def gathered(c, at_centre):
        rows = slice(c * STEP, (c + 1) * STEP)

        @pl.when(has_outer)
        def _():
            up(c).wait_recv()
            acc[:, rows, :] = rho[:, rows, :] + from_outer[:, rows, :]

        @pl.when(jnp.logical_not(has_outer))
        def _():
            acc[:, rows, :] = rho[:, rows, :]

        (mid(c) if at_centre else up(c)).start()

    def spread(c, at_centre):
        rows = slice(c * STEP, (c + 1) * STEP)
        if at_centre:
            mid(c).wait_recv()
            fx[OWN:OWN + PLANES, PAD + c * STEP:PAD + (c + 1) * STEP, :] = (
                acc[:, rows, :] + from_inner[:, rows, :]
            )
        else:
            down(c, inner).wait_recv()

        @pl.when(has_outer)
        def _():
            down(c, outer).start()

        @pl.when(d < domains - 1)
        def _():
            near_up(c).start()

        @pl.when(d > 0)
        def _():
            near_down(c).start()

        if (c + 1) % (CHUNKS // HALVES) == 0:
            for i in range(4):
                @pl.when(far[i][3])
                def _():
                    far_copy(i, c // (CHUNKS // HALVES)).start()

    @pl.when(centre)
    def _():
        for c in range(CHUNKS + LAG):
            if c < CHUNKS:
                gathered(c, True)
            if c >= LAG:
                spread(c - LAG, True)

    @pl.when(jnp.logical_not(centre))
    def _():
        for c in range(CHUNKS):
            gathered(c, False)
        for c in range(CHUNKS):
            spread(c, False)

    for c in range(CHUNKS):
        @pl.when(d < domains - 1)
        def _():
            near_down(c).wait_recv()

        @pl.when(d > 0)
        def _():
            near_up(c).wait_recv()

    def beside(src, p, r0, rn, width):
        c = src[p, PAD + r0:PAD + r0 + rn, :]
        lane = lax.broadcasted_iota(jnp.int32, (rn, NX), 1)
        total = src[p, PAD + r0 - 1:PAD + r0 + rn - 1, :] + src[p, PAD + r0 + 1:PAD + r0 + rn + 1, :]
        total = total + (src[p - 1, PAD + r0:PAD + r0 + rn, :] + src[p + 1, PAD + r0:PAD + r0 + rn, :])
        total = total + jnp.where(lane < width, 0.0, pltpu.roll(c, width, 1))
        total = total + jnp.where(lane >= NX - width, 0.0, pltpu.roll(c, NX - width, 1))
        return c, total

    def rows_of(level):
        return NY >> level

    def blocks(level):
        rn = 48 if rows_of(level) % 48 == 0 else rows_of(level)
        return [(r0, rn) for r0 in range(0, rows_of(level), rn)]

    def loop(lo, count, fn, most=4):
        group = max(n for n in range(1, most + 1) if count % n == 0)

        def step(i, carry):
            for j in range(group):
                fn(lo + i * group + j, j)
            return carry

        lax.fori_loop(0, count // group, step, 0)

    def gain(level, p):
        if level:
            return GAIN[level]
        z = PLANES * d - OWN + p
        inside = jnp.logical_and(z >= 0, z < PLANES * domains)
        return jnp.where(inside, jnp.float32(GAIN[0]), jnp.float32(0.0))

    def first(src, dst, level, lo, count):
        def plane(p, j):
            k = gain(level, p)
            for r0, rn in blocks(level):
                c, total = beside(src, p, r0, rn, 1 << level)
                dst[p, PAD + r0:PAD + r0 + rn, :] = (GAIN[level] * (1.0 + KEEP)) * c + (k * GAIN[level]) * total

        loop(lo, count, plane, MOST[level])

    def sweep(src, source, dst, level, lo, count):
        def plane(p, j):
            k = gain(level, p)
            for r0, rn in blocks(level):
                c, total = beside(src, p, r0, rn, 1 << level)
                f = source[p, PAD + r0:PAD + r0 + rn, :]
                dst[p, PAD + r0:PAD + r0 + rn, :] = KEEP * c + k * (f + total)

        loop(lo, count, plane, MOST[level])

    def residual(v, source, level, p, r0, rn):
        c, total = beside(v, p, r0, rn, 1 << level)
        return source[p, PAD + r0:PAD + r0 + rn, :] + total - CENTRE[level] * c

    spare = (t0, t1, t2, t3)

    def pooled(v, source, level, p, t):
        for r0, rn in blocks(level):
            t[r0:r0 + rn, :] = residual(v, source, level, p, r0, rn) + residual(v, source, level, p + 1, r0, rn)
        n = rows_of(level) // 2
        return t[pl.ds(0, n, stride=2), :] + t[pl.ds(1, n, stride=2), :]

    def window(h):
        return OWN - h, PLANES + 2 * h

    rows1 = NY // 2
    even = lax.broadcasted_iota(jnp.int32, (rows1, NX), 1) % 2 == 0

    def give(cycle, i):
        return remote(
            g.at[cycle, d], g.at[cycle, d], g_s.at[cycle, i], g_r.at[cycle, i],
            (b, lax.rem(d + i, domains)),
        )

    def take(cycle, i):
        origin = lax.rem(d + (domains - i), domains)
        return origin, remote(
            g.at[cycle, origin], g.at[cycle, origin], g_s.at[cycle, i], g_r.at[cycle, i], (b, origin)
        )

    def restrict_and_send(v, cycle):
        a = pooled(v, fx, 0, OWN, t0)
        a = a + pltpu.roll(a, NX - 1, 1)
        e = pooled(v, fx, 0, OWN + 2, t1)
        e = e + pltpu.roll(e, 1, 1)
        g[cycle, d] = 0.5 * jnp.where(even, a, e)
        for i in range(1, domains):
            give(cycle, i).start()

    def unpack(cycle, origin):
        a = g[cycle, origin]
        f1[1 + 2 * origin, PAD:PAD + rows1, :] = jnp.where(even, a, pltpu.roll(a, 1, 1))
        f1[2 + 2 * origin, PAD:PAD + rows1, :] = jnp.where(even, pltpu.roll(a, NX - 1, 1), a)

    def widen(a, level):
        width = 1 << level
        lane = lax.broadcasted_iota(jnp.int32, a.shape, 1)
        low = (lane // width) % 2 == 0
        return 0.5 * (a + jnp.where(low, pltpu.roll(a, NX - width, 1), pltpu.roll(a, width, 1)))

    def add_rows(dst, p, value, n):
        for odd in range(2):
            at = (p, pl.ds(PAD + odd, n, stride=2), slice(None))
            dst[at] = dst[at] + value

    def coarse(cycle, near):
        unpack(cycle, d)
        for i in range(1, domains):
            origin, copy = take(cycle, i)
            copy.wait_recv()
            unpack(cycle, origin)
        first(f1, u1a, 1, 1, n1)

        def down1(q, j):
            f2[1 + q, PAD:PAD + NY // 4, :] = widen(pooled(u1a, f1, 1, 1 + 2 * q, spare[j]), 1)

        loop(0, n2, down1)
        first(f2, u2a, 2, 1, n2)
        rows3 = NY // 8

        def down2(q, j):
            f3[pl.ds(pl.multiple_of(q * rows3, 8), rows3), :] = widen(pooled(u2a, f2, 2, 1 + 2 * q, spare[j]), 2)

        loop(0, n3, down2)
        dot = functools.partial(
            jnp.dot, precision=lax.Precision.HIGHEST, preferred_element_type=jnp.float32
        )
        modes = dot(left[...], dot(f3[...], into[...])) * weight[...]
        f3[...] = dot(dot(left[...], modes), back[...])

        def back2(q, j):
            value = f3[pl.ds(pl.multiple_of(q * rows3, 8), rows3), :]
            add_rows(u2a, 1 + 2 * q, value, rows3)
            add_rows(u2a, 2 + 2 * q, value, rows3)

        loop(0, n3, back2)
        sweep(u2a, f2, u2b, 2, 1, n2)
        sweep(u2b, f2, u2a, 2, 1, n2)

        def back1(q, j):
            value = u2a[1 + q, PAD:PAD + NY // 4, :]
            add_rows(u1a, 1 + 2 * q, value, NY // 4)
            add_rows(u1a, 2 + 2 * q, value, NY // 4)

        loop(0, n2, back1)
        for extra, src, dst in ((1, u1a, u1b), (0, u1b, u1a)):
            count = min(n1, 2 + 2 * (near + extra))
            start = jnp.clip(2 * d - near - extra, 0, n1 - count)
            sweep(src, f1, dst, 1, start + 1, count)

    def correct(v, near):
        for j in range(-near, 2 + near):
            z = 2 * d + j
            w = 2 * j + OWN

            @pl.when(jnp.logical_and(z >= 0, z < n1))
            def _():
                value = u1a[z + 1, PAD:PAD + rows1, :]
                add_rows(v, w, value, rows1)
                add_rows(v, w + 1, value, rows1)

    for i in range(2):
        @pl.when(onward[i][4])
        def _():
            for h in range(HALVES):
                onward_copy(i, h).start()

    first(fx, vb, 0, *window(1))
    restrict_and_send(vb, 0)
    coarse(0, 3)

    for i in range(4):
        @pl.when(far[i][4])
        def _():
            for h in range(HALVES):
                far_copy(i, h).wait_recv()

    first(fx, vb, 0, OWN - 5, 4)
    first(fx, vb, 0, OWN + PLANES + 1, 4)
    correct(vb, 3)
    sweep(vb, fx, va, 0, *window(4))
    sweep(va, fx, vb, 0, *window(3))

    sweep(vb, fx, va, 0, *window(2))
    sweep(va, fx, vc, 0, *window(1))
    restrict_and_send(vc, 1)

    def v_up():
        return remote(
            vc.at[pl.ds(OWN + 2, 2), pl.ds(PAD, NY), :], hv.at[0], hv_s.at[0], hv_r.at[0], (b, d + 1)
        )

    def v_down():
        return remote(
            vc.at[pl.ds(OWN, 2), pl.ds(PAD, NY), :], hv.at[1], hv_s.at[1], hv_r.at[1], (b, d - 1)
        )

    @pl.when(d < domains - 1)
    def _():
        v_up().start()

    @pl.when(d > 0)
    def _():
        v_down().start()

    coarse(1, 1)

    @pl.when(d < domains - 1)
    def _():
        v_up().wait_send()
        v_down().wait_recv()
        vc[OWN + 4:OWN + 6, PAD:PAD + NY, :] = hv[1]

    @pl.when(d > 0)
    def _():
        v_down().wait_send()
        v_up().wait_recv()
        vc[OWN - 2:OWN, PAD:PAD + NY, :] = hv[0]

    correct(vc, 1)
    sweep(vc, fx, va, 0, *window(1))
    for p in range(PLANES):
        for r0, rn in blocks(0):
            c, total = beside(va, OWN + p, r0, rn, 1)
            f = fx[OWN + p, PAD + r0:PAD + r0 + rn, :]
            out[p, r0:r0 + rn, :] = KEEP * c + GAIN[0] * (f + total)

    for c in range(CHUNKS):
        @pl.when(centre)
        def _():
            mid(c).wait_send()

        @pl.when(jnp.logical_not(centre))
        def _():
            up(c).wait_send()

        @pl.when(has_outer)
        def _():
            down(c, outer).wait_send()

        @pl.when(d < domains - 1)
        def _():
            near_up(c).wait_send()

        @pl.when(d > 0)
        def _():
            near_down(c).wait_send()

    for i in range(4):
        @pl.when(far[i][3])
        def _():
            for h in range(HALVES):
                far_copy(i, h).wait_send()

    for i in range(2):
        @pl.when(onward[i][4])
        def _():
            for h in range(HALVES):
                onward_copy(i, h).wait_send()

    for cycle in range(2):
        for i in range(1, domains):
            give(cycle, i).wait_send()


def potential_of(rho, bands, domains):
    n1, n2, n3 = 2 * domains, domains, domains // 2
    tables = coarse_basis(n3)
    f32 = jnp.float32
    slab = pltpu.VMEM((PLANES, NY, NX), f32)
    fine = pltpu.VMEM((WINDOW, NY + 2 * PAD, NX), f32)
    level1 = pltpu.VMEM((n1 + 2, NY // 2 + 2 * PAD, NX), f32)
    level2 = pltpu.VMEM((n2 + 2, NY // 4 + 2 * PAD, NX), f32)
    chunk_sems = pltpu.SemaphoreType.DMA((CHUNKS,))
    near_sems = pltpu.SemaphoreType.DMA((2, CHUNKS))
    gather_sems = pltpu.SemaphoreType.DMA((2, domains))
    vmem = pl.BlockSpec(memory_space=pltpu.VMEM)
    return pl.pallas_call(
        functools.partial(kernel, bands, domains),
        out_shape=jax.ShapeDtypeStruct((PLANES, NY, NX), f32),
        in_specs=[vmem] * 5,
        out_specs=vmem,
        scratch_shapes=[
            slab, slab, slab, fine, fine, fine, fine,
            pltpu.VMEM((2, 2, NY, NX), f32),
            *[pltpu.VMEM((NY, NX), f32)] * 4,
            pltpu.VMEM((2, domains, NY // 2, NX), f32),
            level1, level1, level1, level2, level2, level2,
            pltpu.VMEM((n3 * (NY // 8), NX), f32),
            chunk_sems, chunk_sems, chunk_sems, chunk_sems, chunk_sems, chunk_sems,
            near_sems, near_sems,
            pltpu.SemaphoreType.DMA((6, HALVES)), pltpu.SemaphoreType.DMA((4, HALVES)),
            pltpu.SemaphoreType.DMA((2,)), pltpu.SemaphoreType.DMA((2,)),
            gather_sems, gather_sems,
        ],
        compiler_params=pltpu.CompilerParams(
            collective_id=0, has_side_effects=True, vmem_limit_bytes=48 * 1024 * 1024
        ),
    )(rho, *[jnp.asarray(table) for table in tables])


def body(bands, domains, orbitals, occupations):
    planes = orbitals.shape[1]
    orbital_total = orbitals.shape[0] * bands
    weights = occupations.astype(jnp.float32) * (0.5 * charge_scale / orbital_total)
    values = orbitals.astype(jnp.float32)
    rho = jnp.sum(weights[:, None, None] * (values * values), axis=0)
    potential = potential_of(rho.reshape(planes, NY, NX), bands, domains)
    potential = potential.reshape(planes, NY * NX)
    applied = (potential[None] * values).astype(jnp.bfloat16)
    return (potential, applied)


def solution(mesh):
    return jax.shard_map(
        functools.partial(body, mesh.shape["band"], mesh.shape["dom"]),
        mesh=mesh,
        in_specs=(P("band", "dom", None), P("band")),
        out_specs=(P("dom", None), P("band", "dom", None)),
        check_vma=False,
    )
```

```python
import functools

import jax
import jax.numpy as jnp
import numpy as np
from jax import lax
from jax.experimental import pallas as pl
from jax.experimental.pallas import tpu as pltpu
from jax.sharding import PartitionSpec as P

NX = 128
NY = 192
COARSE = 48

screening = 0.02
relaxation = 0.8
charge_scale = 0.07

PLANES = 4
HALO = 6
OWN = HALO
WINDOW = PLANES + 2 * HALO
PAD = 8
CHUNKS = 8
LAG = 3
AHEAD = 2
HALVES = 2
MOST = (4, 4, 8)
STEP = NY // CHUNKS
HALF = NY // HALVES
CENTRE = [6.0 + screening * 4.0**level for level in range(4)]
GAIN = [relaxation / centre for centre in CENTRE]
KEEP = 1.0 - relaxation


def sines(n):
    k = np.arange(1, n + 1)
    basis = np.sqrt(2.0 / (n + 1)) * np.sin(np.pi * np.outer(k, k) / (n + 1))
    return basis, 2.0 * np.cos(np.pi * k / (n + 1))


def coarse_basis(depth):
    rows, cols, copies = NY // 8, NX // 8, 8
    sz, ez = sines(depth)
    sy, ey = sines(rows)
    sx, ex = sines(cols)
    left = np.kron(sz, sy)
    into = np.zeros((NX, NX))
    into[::copies, :cols] = sx
    back = np.zeros((NX, NX))
    back[:cols] = np.repeat(sx, copies, axis=1)
    near = (ez[:, None] + ey[None, :]).reshape(-1, 1) + ex[None, :]
    rate = KEEP + GAIN[3] * near
    total = GAIN[3] * sum(rate**n for n in range(COARSE))
    weight = np.zeros((depth * rows, NX))
    weight[:, :cols] = total
    return [np.asarray(part, np.float32) for part in (left, into, back, weight)]


def kernel(
    bands, domains, scale,
    occupations, orbitals, left_in, into_in, back_in, weight_in,
    out,
    occ, left, into, back, weight, held, mixed, out_s, table_s, held_s,
    acc, from_outer, from_inner, fx, va, vb, vc, hv, t0, t1, t2, t3, g,
    f1, u1a, u1b, f2, u2a, u2b, f3,
    up_s, up_r, mid_s, mid_r, down_s, down_r, near_s, near_r, far_s, far_r, hv_s, hv_r, g_s, g_r,
):
    b = lax.axis_index("band")
    d = lax.axis_index("dom")
    half = bands // 2
    lower = b < half
    inner = jnp.where(lower, b + 1, b - 1)
    outer = jnp.where(lower, b - 1, b + 1)
    has_outer = jnp.logical_and(b > 0, b < bands - 1)
    centre = jnp.logical_or(b == half - 1, b == half)
    n1, n2, n3 = 2 * domains, domains, domains // 2

    def remote(src, dst, ss, rs, dev):
        return pltpu.make_async_remote_copy(
            src_ref=src, dst_ref=dst, send_sem=ss, recv_sem=rs,
            device_id=dev, device_id_type=pl.DeviceIdType.MESH,
        )

    lanes = STEP * NX

    def fetch(c):
        at = (slice(None), slice(None), pl.ds(c * lanes, lanes))
        return pltpu.make_async_copy(orbitals.at[at], held.at[at], held_s.at[c])

    def result(p):
        return pltpu.make_async_copy(acc.at[p], out.at[p], out_s.at[p])

    tables = [
        pltpu.make_async_copy(src, dst, table_s.at[i])
        for i, (src, dst) in enumerate(
            ((occupations, occ), (left_in, left), (into_in, into), (back_in, back), (weight_in, weight))
        )
    ]
    tables[0].start()
    for c in range(CHUNKS):
        fetch(c).start()
    for table in tables[1:]:
        table.start()
    barrier = pltpu.get_barrier_semaphore()

    def greet(dev):
        pl.semaphore_signal(barrier, inc=1, device_id=dev, device_id_type=pl.DeviceIdType.MESH)

    for i in range(1, domains):
        greet((b, lax.rem(d + i, domains)))
    greet((inner, d))

    @pl.when(has_outer)
    def _():
        greet((outer, d))

    for ref in (fx, va, vb, vc, f1, u1a, u1b, f2, u2a, u2b):
        edge = jnp.zeros((ref.shape[0], PAD, NX), jnp.float32)
        ref[:, 0:PAD, :] = edge
        ref[:, ref.shape[1] - PAD:ref.shape[1], :] = edge

    def clear(ref, p):
        ref[p] = jnp.zeros(ref.shape[1:], jnp.float32)

    for ref in (f1, u1a, u1b, f2, u2a, u2b):
        clear(ref, 0)
        clear(ref, ref.shape[0] - 1)
    clear(vc, OWN - 2)
    clear(vc, OWN + 5)
    for k in range(HALO):
        reach = -(-(HALO - k) // PLANES)

        @pl.when(d < reach)
        def _():
            clear(fx, k)

        @pl.when(d >= domains - reach)
        def _():
            clear(fx, WINDOW - 1 - k)

    def density(c):
        fetch(c).wait()
        total = None
        for i in range(orbitals.shape[0]):
            value = held[i, :, c * lanes:(c + 1) * lanes].astype(jnp.float32)
            term = (occ[i].astype(jnp.float32) * scale) * (value * value)
            total = term if total is None else total + term
        first_row = c * STEP * PLANES
        for y in range(STEP):
            at = first_row + y * PLANES
            mixed[at:at + PLANES, :] = total[:, y * NX:(y + 1) * NX]
        for p in range(PLANES):
            acc[p, c * STEP:(c + 1) * STEP, :] = mixed[pl.ds(first_row + p, STEP, stride=PLANES), :]

    tables[0].wait()
    for c in range(AHEAD):
        density(c)
    pl.semaphore_wait(barrier, domains + jnp.where(has_outer, 1, 0))

    def part(ref, c):
        return ref.at[:, pl.ds(c * STEP, STEP), :]

    def slab(c):
        return fx.at[pl.ds(OWN, PLANES), pl.ds(PAD + c * STEP, STEP), :]

    def up(c):
        return remote(part(acc, c), part(from_outer, c), up_s.at[c], up_r.at[c], (inner, d))

    def mid(c):
        return remote(part(acc, c), part(from_inner, c), mid_s.at[c], mid_r.at[c], (inner, d))

    def down(c, dev):
        return remote(slab(c), slab(c), down_s.at[c], down_r.at[c], (dev, d))

    def near_up(c):
        rows = pl.ds(PAD + c * STEP, STEP)
        return remote(
            fx.at[pl.ds(OWN + 2, 2), rows, :], fx.at[pl.ds(OWN - 2, 2), rows, :],
            near_s.at[0, c], near_r.at[0, c], (b, d + 1),
        )

    def near_down(c):
        rows = pl.ds(PAD + c * STEP, STEP)
        return remote(
            fx.at[pl.ds(OWN, 2), rows, :], fx.at[pl.ds(OWN + 4, 2), rows, :],
            near_s.at[1, c], near_r.at[1, c], (b, d - 1),
        )

    even_d = lax.rem(d, 2) == 0
    odd_d = lax.rem(d, 2) == 1
    far = [
        (OWN, OWN - 4, 1, d < domains - 1, d > 0),
        (OWN + 2, OWN + 6, -1, d > 0, d < domains - 1),
        (OWN + 2, OWN - 6, 2, jnp.logical_and(even_d, d < domains - 2), d > 1),
        (OWN, OWN + 8, -2, jnp.logical_and(odd_d, d > 1), d < domains - 2),
    ]

    def far_copy(i, h):
        at, to, offset, _, _ = far[i]
        rows = pl.ds(PAD + h * HALF, HALF)
        return remote(
            fx.at[pl.ds(at, 2), rows, :], fx.at[pl.ds(to, 2), rows, :],
            far_s.at[i, h], far_r.at[i, h], (b, d + offset),
        )

    onward = [
        (OWN - 2, OWN - 6, 1, 2, jnp.logical_and(even_d, d > 1)),
        (OWN + 4, OWN + 8, -1, 3, jnp.logical_and(odd_d, d < domains - 2)),
    ]

    def onward_copy(i, h):
        at, to, offset, slot, _ = onward[i]
        rows = pl.ds(PAD + h * HALF, HALF)
        return remote(
            fx.at[pl.ds(at, 2), rows, :], fx.at[pl.ds(to, 2), rows, :],
            far_s.at[slot + 2, h], far_r.at[slot, h], (b, d + offset),
        )

    def gathered(c, at_centre):
        rows = slice(c * STEP, (c + 1) * STEP)

        if c >= AHEAD:
            density(c)

        @pl.when(has_outer)
        def _():
            up(c).wait_recv()
            acc[:, rows, :] = acc[:, rows, :] + from_outer[:, rows, :]

        (mid(c) if at_centre else up(c)).start()

    def spread(c, at_centre):
        rows = slice(c * STEP, (c + 1) * STEP)
        if at_centre:
            mid(c).wait_recv()
            fx[OWN:OWN + PLANES, PAD + c * STEP:PAD + (c + 1) * STEP, :] = (
                acc[:, rows, :] + from_inner[:, rows, :]
            )
        else:
            down(c, inner).wait_recv()

        @pl.when(has_outer)
        def _():
            down(c, outer).start()

        @pl.when(d < domains - 1)
        def _():
            near_up(c).start()

        @pl.when(d > 0)
        def _():
            near_down(c).start()

        if (c + 1) % (CHUNKS // HALVES) == 0:
            for i in range(4):
                @pl.when(far[i][3])
                def _():
                    far_copy(i, c // (CHUNKS // HALVES)).start()

    @pl.when(centre)
    def _():
        for c in range(CHUNKS + LAG):
            if c < CHUNKS:
                gathered(c, True)
            if c >= LAG:
                spread(c - LAG, True)

    @pl.when(jnp.logical_not(centre))
    def _():
        for c in range(CHUNKS):
            gathered(c, False)
        for c in range(CHUNKS):
            spread(c, False)

    for c in range(CHUNKS):
        @pl.when(d < domains - 1)
        def _():
            near_down(c).wait_recv()

        @pl.when(d > 0)
        def _():
            near_up(c).wait_recv()

    def beside(src, p, r0, rn, width):
        c = src[p, PAD + r0:PAD + r0 + rn, :]
        lane = lax.broadcasted_iota(jnp.int32, (rn, NX), 1)
        total = src[p, PAD + r0 - 1:PAD + r0 + rn - 1, :] + src[p, PAD + r0 + 1:PAD + r0 + rn + 1, :]
        total = total + (src[p - 1, PAD + r0:PAD + r0 + rn, :] + src[p + 1, PAD + r0:PAD + r0 + rn, :])
        total = total + jnp.where(lane < width, 0.0, pltpu.roll(c, width, 1))
        total = total + jnp.where(lane >= NX - width, 0.0, pltpu.roll(c, NX - width, 1))
        return c, total

    def rows_of(level):
        return NY >> level

    def blocks(level):
        rn = 48 if rows_of(level) % 48 == 0 else rows_of(level)
        return [(r0, rn) for r0 in range(0, rows_of(level), rn)]

    def loop(lo, count, fn, most=4):
        group = max(n for n in range(1, most + 1) if count % n == 0)

        def step(i, carry):
            for j in range(group):
                fn(lo + i * group + j, j)
            return carry

        lax.fori_loop(0, count // group, step, 0)

    def gain(level, p):
        if level:
            return GAIN[level]
        z = PLANES * d - OWN + p
        inside = jnp.logical_and(z >= 0, z < PLANES * domains)
        return jnp.where(inside, jnp.float32(GAIN[0]), jnp.float32(0.0))

    def first(src, dst, level, lo, count):
        def plane(p, j):
            k = gain(level, p)
            for r0, rn in blocks(level):
                c, total = beside(src, p, r0, rn, 1 << level)
                dst[p, PAD + r0:PAD + r0 + rn, :] = (GAIN[level] * (1.0 + KEEP)) * c + (k * GAIN[level]) * total

        loop(lo, count, plane, MOST[level])

    def sweep(src, source, dst, level, lo, count):
        def plane(p, j):
            k = gain(level, p)
            for r0, rn in blocks(level):
                c, total = beside(src, p, r0, rn, 1 << level)
                f = source[p, PAD + r0:PAD + r0 + rn, :]
                dst[p, PAD + r0:PAD + r0 + rn, :] = KEEP * c + k * (f + total)

        loop(lo, count, plane, MOST[level])

    def residual(v, source, level, p, r0, rn):
        c, total = beside(v, p, r0, rn, 1 << level)
        return source[p, PAD + r0:PAD + r0 + rn, :] + total - CENTRE[level] * c

    spare = (t0, t1, t2, t3)

    def pooled(v, source, level, p, t):
        for r0, rn in blocks(level):
            t[r0:r0 + rn, :] = residual(v, source, level, p, r0, rn) + residual(v, source, level, p + 1, r0, rn)
        n = rows_of(level) // 2
        return t[pl.ds(0, n, stride=2), :] + t[pl.ds(1, n, stride=2), :]

    def window(h):
        return OWN - h, PLANES + 2 * h

    rows1 = NY // 2
    even = lax.broadcasted_iota(jnp.int32, (rows1, NX), 1) % 2 == 0

    def give(cycle, i):
        return remote(
            g.at[cycle, d], g.at[cycle, d], g_s.at[cycle, i], g_r.at[cycle, i],
            (b, lax.rem(d + i, domains)),
        )

    def take(cycle, i):
        origin = lax.rem(d + (domains - i), domains)
        return origin, remote(
            g.at[cycle, origin], g.at[cycle, origin], g_s.at[cycle, i], g_r.at[cycle, i], (b, origin)
        )

    def restrict_and_send(v, cycle):
        a = pooled(v, fx, 0, OWN, t0)
        a = a + pltpu.roll(a, NX - 1, 1)
        e = pooled(v, fx, 0, OWN + 2, t1)
        e = e + pltpu.roll(e, 1, 1)
        g[cycle, d] = 0.5 * jnp.where(even, a, e)
        for i in range(1, domains):
            give(cycle, i).start()

    def unpack(cycle, origin):
        a = g[cycle, origin]
        f1[1 + 2 * origin, PAD:PAD + rows1, :] = jnp.where(even, a, pltpu.roll(a, 1, 1))
        f1[2 + 2 * origin, PAD:PAD + rows1, :] = jnp.where(even, pltpu.roll(a, NX - 1, 1), a)

    def widen(a, level):
        width = 1 << level
        lane = lax.broadcasted_iota(jnp.int32, a.shape, 1)
        low = (lane // width) % 2 == 0
        return 0.5 * (a + jnp.where(low, pltpu.roll(a, NX - width, 1), pltpu.roll(a, width, 1)))

    def add_rows(dst, p, value, n):
        for odd in range(2):
            at = (p, pl.ds(PAD + odd, n, stride=2), slice(None))
            dst[at] = dst[at] + value

    def coarse(cycle, near):
        unpack(cycle, d)
        for i in range(1, domains):
            origin, copy = take(cycle, i)
            copy.wait_recv()
            unpack(cycle, origin)
        first(f1, u1a, 1, 1, n1)

        def down1(q, j):
            f2[1 + q, PAD:PAD + NY // 4, :] = widen(pooled(u1a, f1, 1, 1 + 2 * q, spare[j]), 1)

        loop(0, n2, down1)
        first(f2, u2a, 2, 1, n2)
        rows3 = NY // 8

        def down2(q, j):
            f3[pl.ds(pl.multiple_of(q * rows3, 8), rows3), :] = widen(pooled(u2a, f2, 2, 1 + 2 * q, spare[j]), 2)

        loop(0, n3, down2)
        dot = functools.partial(
            jnp.dot, precision=lax.Precision.HIGHEST, preferred_element_type=jnp.float32
        )
        modes = dot(left[...], dot(f3[...], into[...])) * weight[...]
        f3[...] = dot(dot(left[...], modes), back[...])

        def back2(q, j):
            value = f3[pl.ds(pl.multiple_of(q * rows3, 8), rows3), :]
            add_rows(u2a, 1 + 2 * q, value, rows3)
            add_rows(u2a, 2 + 2 * q, value, rows3)

        loop(0, n3, back2)
        sweep(u2a, f2, u2b, 2, 1, n2)
        sweep(u2b, f2, u2a, 2, 1, n2)

        def back1(q, j):
            value = u2a[1 + q, PAD:PAD + NY // 4, :]
            add_rows(u1a, 1 + 2 * q, value, NY // 4)
            add_rows(u1a, 2 + 2 * q, value, NY // 4)

        loop(0, n2, back1)
        for extra, src, dst in ((1, u1a, u1b), (0, u1b, u1a)):
            count = min(n1, 2 + 2 * (near + extra))
            start = jnp.clip(2 * d - near - extra, 0, n1 - count)
            sweep(src, f1, dst, 1, start + 1, count)

    def correct(v, near):
        for j in range(-near, 2 + near):
            z = 2 * d + j
            w = 2 * j + OWN

            @pl.when(jnp.logical_and(z >= 0, z < n1))
            def _():
                value = u1a[z + 1, PAD:PAD + rows1, :]
                add_rows(v, w, value, rows1)
                add_rows(v, w + 1, value, rows1)

    for i in range(2):
        @pl.when(onward[i][4])
        def _():
            for h in range(HALVES):
                onward_copy(i, h).start()

    first(fx, vb, 0, *window(1))
    restrict_and_send(vb, 0)
    for table in tables[1:]:
        table.wait()
    coarse(0, 3)

    for i in range(4):
        @pl.when(far[i][4])
        def _():
            for h in range(HALVES):
                far_copy(i, h).wait_recv()

    first(fx, vb, 0, OWN - 5, 4)
    first(fx, vb, 0, OWN + PLANES + 1, 4)
    correct(vb, 3)
    sweep(vb, fx, va, 0, *window(4))
    sweep(va, fx, vb, 0, *window(3))

    sweep(vb, fx, va, 0, *window(2))
    sweep(va, fx, vc, 0, *window(1))
    restrict_and_send(vc, 1)

    def v_up():
        return remote(
            vc.at[pl.ds(OWN + 2, 2), pl.ds(PAD, NY), :], hv.at[0], hv_s.at[0], hv_r.at[0], (b, d + 1)
        )

    def v_down():
        return remote(
            vc.at[pl.ds(OWN, 2), pl.ds(PAD, NY), :], hv.at[1], hv_s.at[1], hv_r.at[1], (b, d - 1)
        )

    @pl.when(d < domains - 1)
    def _():
        v_up().start()

    @pl.when(d > 0)
    def _():
        v_down().start()

    coarse(1, 1)

    @pl.when(d < domains - 1)
    def _():
        v_up().wait_send()
        v_down().wait_recv()
        vc[OWN + 4:OWN + 6, PAD:PAD + NY, :] = hv[1]

    @pl.when(d > 0)
    def _():
        v_down().wait_send()
        v_up().wait_recv()
        vc[OWN - 2:OWN, PAD:PAD + NY, :] = hv[0]

    for c in range(CHUNKS):
        @pl.when(centre)
        def _():
            mid(c).wait_send()

        @pl.when(jnp.logical_not(centre))
        def _():
            up(c).wait_send()

    correct(vc, 1)
    sweep(vc, fx, va, 0, *window(1))
    for p in range(PLANES):
        for r0, rn in blocks(0):
            c, total = beside(va, OWN + p, r0, rn, 1)
            f = fx[OWN + p, PAD + r0:PAD + r0 + rn, :]
            acc[p, r0:r0 + rn, :] = KEEP * c + GAIN[0] * (f + total)
        result(p).start()
    for p in range(PLANES):
        result(p).wait()

    for c in range(CHUNKS):
        @pl.when(has_outer)
        def _():
            down(c, outer).wait_send()

        @pl.when(d < domains - 1)
        def _():
            near_up(c).wait_send()

        @pl.when(d > 0)
        def _():
            near_down(c).wait_send()

    for i in range(4):
        @pl.when(far[i][3])
        def _():
            for h in range(HALVES):
                far_copy(i, h).wait_send()

    for i in range(2):
        @pl.when(onward[i][4])
        def _():
            for h in range(HALVES):
                onward_copy(i, h).wait_send()

    for cycle in range(2):
        for i in range(1, domains):
            give(cycle, i).wait_send()


def potential_of(orbitals, occupations, bands, domains):
    n1, n2, n3 = 2 * domains, domains, domains // 2
    tables = coarse_basis(n3)
    f32 = jnp.float32
    count = orbitals.shape[0]
    slab = pltpu.VMEM((PLANES, NY, NX), f32)
    fine = pltpu.VMEM((WINDOW, NY + 2 * PAD, NX), f32)
    level1 = pltpu.VMEM((n1 + 2, NY // 2 + 2 * PAD, NX), f32)
    level2 = pltpu.VMEM((n2 + 2, NY // 4 + 2 * PAD, NX), f32)
    chunk_sems = pltpu.SemaphoreType.DMA((CHUNKS,))
    near_sems = pltpu.SemaphoreType.DMA((2, CHUNKS))
    gather_sems = pltpu.SemaphoreType.DMA((2, domains))
    return pl.pallas_call(
        functools.partial(kernel, bands, domains, 0.5 * charge_scale / (count * bands)),
        out_shape=jax.ShapeDtypeStruct((PLANES, NY, NX), f32),
        in_specs=[pl.BlockSpec(memory_space=pl.ANY)] * 6,
        out_specs=pl.BlockSpec(memory_space=pl.ANY),
        scratch_shapes=[
            pltpu.SMEM(occupations.shape, jnp.int32),
            *[pltpu.VMEM(table.shape, f32) for table in tables],
            pltpu.VMEM(orbitals.shape, orbitals.dtype),
            pltpu.VMEM((NY * PLANES, NX), f32),
            pltpu.SemaphoreType.DMA((PLANES,)), pltpu.SemaphoreType.DMA((5,)), chunk_sems,
            slab, slab, slab, fine, fine, fine, fine,
            pltpu.VMEM((2, 2, NY, NX), f32),
            *[pltpu.VMEM((NY, NX), f32)] * 4,
            pltpu.VMEM((2, domains, NY // 2, NX), f32),
            level1, level1, level1, level2, level2, level2,
            pltpu.VMEM((n3 * (NY // 8), NX), f32),
            chunk_sems, chunk_sems, chunk_sems, chunk_sems, chunk_sems, chunk_sems,
            near_sems, near_sems,
            pltpu.SemaphoreType.DMA((6, HALVES)), pltpu.SemaphoreType.DMA((4, HALVES)),
            pltpu.SemaphoreType.DMA((2,)), pltpu.SemaphoreType.DMA((2,)),
            gather_sems, gather_sems,
        ],
        compiler_params=pltpu.CompilerParams(
            collective_id=0, has_side_effects=True, vmem_limit_bytes=62_500_000
        ),
    )(occupations, orbitals, *[jnp.asarray(table) for table in tables])


def body(bands, domains, orbitals, occupations):
    values = orbitals.astype(jnp.float32)
    potential = potential_of(orbitals, occupations, bands, domains).reshape(orbitals.shape[1], NY * NX)
    applied = (potential[None] * values).astype(jnp.bfloat16)
    return (potential, applied)


def solution(mesh):
    return jax.shard_map(
        functools.partial(body, mesh.shape["band"], mesh.shape["dom"]),
        mesh=mesh,
        in_specs=(P("band", "dom", None), P("band")),
        out_specs=(P("dom", None), P("band", "dom", None)),
        check_vma=False,
    )
```

```python
import functools

import jax
import jax.numpy as jnp
import numpy as np
from jax import lax
from jax.experimental import pallas as pl
from jax.experimental.pallas import tpu as pltpu
from jax.sharding import PartitionSpec as P

NX = 128
NY = 192
COARSE = 48

screening = 0.02
relaxation = 0.8
charge_scale = 0.07

PLANES = 4
HALO = 6
OWN = HALO
WINDOW = PLANES + 2 * HALO
PAD = 8
CHUNKS = 8
LAG = 3
EARLY = 2
HALVES = 2
MOST = (4, 4, 8)
STEP = NY // CHUNKS
HALF = NY // HALVES
CENTRE = [6.0 + screening * 4.0**level for level in range(4)]
GAIN = [relaxation / centre for centre in CENTRE]
KEEP = 1.0 - relaxation


def sines(n):
    k = np.arange(1, n + 1)
    basis = np.sqrt(2.0 / (n + 1)) * np.sin(np.pi * np.outer(k, k) / (n + 1))
    return basis, 2.0 * np.cos(np.pi * k / (n + 1))


def coarse_basis(depth):
    rows, cols, copies = NY // 8, NX // 8, 8
    sz, ez = sines(depth)
    sy, ey = sines(rows)
    sx, ex = sines(cols)
    left = np.kron(sz, sy)
    into = np.zeros((NX, NX))
    into[::copies, :cols] = sx
    back = np.zeros((NX, NX))
    back[:cols] = np.repeat(sx, copies, axis=1)
    near = (ez[:, None] + ey[None, :]).reshape(-1, 1) + ex[None, :]
    rate = KEEP + GAIN[3] * near
    total = GAIN[3] * sum(rate**n for n in range(COARSE))
    weight = np.zeros((depth * rows, NX))
    weight[:, :cols] = total
    return [np.asarray(part, np.float32) for part in (left, into, back, weight)]


def kernel(
    bands, domains, scale,
    occupations, orbitals, left_in, into_in, back_in, weight_in,
    out,
    occ, left, into, back, weight, held, mixed, out_s, table_s, held_s,
    acc, from_outer, from_inner, fx, va, vb, vc, hv, t0, t1, t2, t3, g,
    share, share_outer, share_inner, shares,
    f1, u1a, u1b, f2, u2a, u2b, f3,
    up_s, up_r, mid_s, mid_r, down_s, down_r, near_s, near_r, far_s, far_r, hv_s, hv_r, g_s, g_r,
    sum_s, sum_r, share_s, share_r, pass_s, pass_r,
):
    b = lax.axis_index("band")
    d = lax.axis_index("dom")
    half = bands // 2
    lower = b < half
    inner = jnp.where(lower, b + 1, b - 1)
    outer = jnp.where(lower, b - 1, b + 1)
    has_outer = jnp.logical_and(b > 0, b < bands - 1)
    centre = jnp.logical_or(b == half - 1, b == half)
    n1, n2, n3 = 2 * domains, domains, domains // 2

    def remote(src, dst, ss, rs, dev):
        return pltpu.make_async_remote_copy(
            src_ref=src, dst_ref=dst, send_sem=ss, recv_sem=rs,
            device_id=dev, device_id_type=pl.DeviceIdType.MESH,
        )

    lanes = STEP * NX

    def fetch(c):
        at = (slice(None), slice(None), pl.ds(c * lanes, lanes))
        return pltpu.make_async_copy(orbitals.at[at], held.at[at], held_s.at[c])

    def result(p):
        return pltpu.make_async_copy(acc.at[p], out.at[p], out_s.at[p])

    tables = [
        pltpu.make_async_copy(src, dst, table_s.at[i])
        for i, (src, dst) in enumerate(
            ((occupations, occ), (left_in, left), (into_in, into), (back_in, back), (weight_in, weight))
        )
    ]
    tables[0].start()
    for c in range(CHUNKS):
        fetch(c).start()
    for table in tables[1:]:
        table.start()
    barrier = pltpu.get_barrier_semaphore()

    def greet(dev):
        pl.semaphore_signal(barrier, inc=1, device_id=dev, device_id_type=pl.DeviceIdType.MESH)

    for i in range(1, domains):
        greet((b, lax.rem(d + i, domains)))
    greet((inner, d))

    @pl.when(has_outer)
    def _():
        greet((outer, d))

    for ref in (fx, va, vb, vc, f1, u1a, u1b, f2, u2a, u2b):
        edge = jnp.zeros((ref.shape[0], PAD, NX), jnp.float32)
        ref[:, 0:PAD, :] = edge
        ref[:, ref.shape[1] - PAD:ref.shape[1], :] = edge

    def clear(ref, p):
        ref[p] = jnp.zeros(ref.shape[1:], jnp.float32)

    for ref in (f1, u1a, u1b, f2, u2a, u2b):
        clear(ref, 0)
        clear(ref, ref.shape[0] - 1)
    clear(vc, OWN - 2)
    clear(vc, OWN + 5)
    for p in (OWN - 2, OWN - 1, OWN + 4, OWN + 5):
        clear(va, p)
    for p in (OWN - 3, OWN - 2, OWN + 5, OWN + 6):
        clear(vb, p)
    for k in range(HALO):
        reach = -(-(HALO - k) // PLANES)

        @pl.when(d < reach)
        def _():
            clear(fx, k)

        @pl.when(d >= domains - reach)
        def _():
            clear(fx, WINDOW - 1 - k)

    def density(c):
        fetch(c).wait()
        total = None
        for i in range(orbitals.shape[0]):
            value = held[i, :, c * lanes:(c + 1) * lanes].astype(jnp.float32)
            term = (occ[i].astype(jnp.float32) * scale) * (value * value)
            total = term if total is None else total + term
        first_row = c * STEP * PLANES
        for y in range(STEP):
            at = first_row + y * PLANES
            mixed[at:at + PLANES, :] = total[:, y * NX:(y + 1) * NX]
        for p in range(PLANES):
            plane = mixed[pl.ds(first_row + p, STEP, stride=PLANES), :]
            acc[p, c * STEP:(c + 1) * STEP, :] = plane
            va[OWN + p, PAD + c * STEP:PAD + (c + 1) * STEP, :] = plane

    tables[0].wait()
    for c in range(CHUNKS):
        density(c)
    pl.semaphore_wait(barrier, domains + jnp.where(has_outer, 1, 0))

    def part(ref, c):
        return ref.at[:, pl.ds(c * STEP, STEP), :]

    def slab(c):
        return fx.at[pl.ds(OWN, PLANES), pl.ds(PAD + c * STEP, STEP), :]

    def up(c):
        return remote(part(acc, c), part(from_outer, c), up_s.at[c], up_r.at[c], (inner, d))

    def mid(c):
        return remote(part(acc, c), part(from_inner, c), mid_s.at[c], mid_r.at[c], (inner, d))

    def down(c, dev):
        return remote(slab(c), slab(c), down_s.at[c], down_r.at[c], (dev, d))

    def near_up(c):
        rows = pl.ds(PAD + c * STEP, STEP)
        return remote(
            fx.at[pl.ds(OWN + 2, 2), rows, :], fx.at[pl.ds(OWN - 2, 2), rows, :],
            near_s.at[0, c], near_r.at[0, c], (b, d + 1),
        )

    def near_down(c):
        rows = pl.ds(PAD + c * STEP, STEP)
        return remote(
            fx.at[pl.ds(OWN, 2), rows, :], fx.at[pl.ds(OWN + 4, 2), rows, :],
            near_s.at[1, c], near_r.at[1, c], (b, d - 1),
        )

    even_d = lax.rem(d, 2) == 0
    odd_d = lax.rem(d, 2) == 1
    far = [
        (OWN, OWN - 4, 1, d < domains - 1, d > 0),
        (OWN + 2, OWN + 6, -1, d > 0, d < domains - 1),
        (OWN + 2, OWN - 6, 2, jnp.logical_and(even_d, d < domains - 2), d > 1),
        (OWN, OWN + 8, -2, jnp.logical_and(odd_d, d > 1), d < domains - 2),
    ]

    def far_copy(i, h):
        at, to, offset, _, _ = far[i]
        rows = pl.ds(PAD + h * HALF, HALF)
        return remote(
            fx.at[pl.ds(at, 2), rows, :], fx.at[pl.ds(to, 2), rows, :],
            far_s.at[i, h], far_r.at[i, h], (b, d + offset),
        )

    onward = [
        (OWN - 2, OWN - 6, 1, 2, jnp.logical_and(even_d, d > 1)),
        (OWN + 4, OWN + 8, -1, 3, jnp.logical_and(odd_d, d < domains - 2)),
    ]

    def onward_copy(i, h):
        at, to, offset, slot, _ = onward[i]
        rows = pl.ds(PAD + h * HALF, HALF)
        return remote(
            fx.at[pl.ds(at, 2), rows, :], fx.at[pl.ds(to, 2), rows, :],
            far_s.at[slot + 2, h], far_r.at[slot, h], (b, d + offset),
        )

    def gathered(c, at_centre):
        rows = slice(c * STEP, (c + 1) * STEP)

        @pl.when(has_outer)
        def _():
            up(c).wait_recv()
            acc[:, rows, :] = acc[:, rows, :] + from_outer[:, rows, :]

        (mid(c) if at_centre else up(c)).start()

    def spread(c, at_centre):
        rows = slice(c * STEP, (c + 1) * STEP)
        if at_centre:
            mid(c).wait_recv()
            fx[OWN:OWN + PLANES, PAD + c * STEP:PAD + (c + 1) * STEP, :] = (
                acc[:, rows, :] + from_inner[:, rows, :]
            )
        else:
            down(c, inner).wait_recv()

        @pl.when(has_outer)
        def _():
            down(c, outer).start()

        @pl.when(d < domains - 1)
        def _():
            near_up(c).start()

        @pl.when(d > 0)
        def _():
            near_down(c).start()

        if (c + 1) % (CHUNKS // HALVES) == 0:
            for i in range(4):
                @pl.when(far[i][3])
                def _():
                    far_copy(i, c // (CHUNKS // HALVES)).start()

    def beside(src, p, r0, rn, width):
        c = src[p, PAD + r0:PAD + r0 + rn, :]
        lane = lax.broadcasted_iota(jnp.int32, (rn, NX), 1)
        total = src[p, PAD + r0 - 1:PAD + r0 + rn - 1, :] + src[p, PAD + r0 + 1:PAD + r0 + rn + 1, :]
        total = total + (src[p - 1, PAD + r0:PAD + r0 + rn, :] + src[p + 1, PAD + r0:PAD + r0 + rn, :])
        total = total + jnp.where(lane < width, 0.0, pltpu.roll(c, width, 1))
        total = total + jnp.where(lane >= NX - width, 0.0, pltpu.roll(c, NX - width, 1))
        return c, total

    def rows_of(level):
        return NY >> level

    def blocks(level):
        rn = 48 if rows_of(level) % 48 == 0 else rows_of(level)
        return [(r0, rn) for r0 in range(0, rows_of(level), rn)]

    def loop(lo, count, fn, most=4):
        group = max(n for n in range(1, most + 1) if count % n == 0)

        def step(i, carry):
            for j in range(group):
                fn(lo + i * group + j, j)
            return carry

        lax.fori_loop(0, count // group, step, 0)

    def gain(level, p):
        if level:
            return GAIN[level]
        z = PLANES * d - OWN + p
        inside = jnp.logical_and(z >= 0, z < PLANES * domains)
        return jnp.where(inside, jnp.float32(GAIN[0]), jnp.float32(0.0))

    def first(src, dst, level, lo, count):
        def plane(p, j):
            k = gain(level, p)
            for r0, rn in blocks(level):
                c, total = beside(src, p, r0, rn, 1 << level)
                dst[p, PAD + r0:PAD + r0 + rn, :] = (GAIN[level] * (1.0 + KEEP)) * c + (k * GAIN[level]) * total

        loop(lo, count, plane, MOST[level])

    def sweep(src, source, dst, level, lo, count):
        def plane(p, j):
            k = gain(level, p)
            for r0, rn in blocks(level):
                c, total = beside(src, p, r0, rn, 1 << level)
                f = source[p, PAD + r0:PAD + r0 + rn, :]
                dst[p, PAD + r0:PAD + r0 + rn, :] = KEEP * c + k * (f + total)

        loop(lo, count, plane, MOST[level])

    def residual(v, source, level, p, r0, rn):
        c, total = beside(v, p, r0, rn, 1 << level)
        return source[p, PAD + r0:PAD + r0 + rn, :] + total - CENTRE[level] * c

    spare = (t0, t1, t2, t3)

    def pooled(v, source, level, p, t):
        for r0, rn in blocks(level):
            t[r0:r0 + rn, :] = residual(v, source, level, p, r0, rn) + residual(v, source, level, p + 1, r0, rn)
        n = rows_of(level) // 2
        return t[pl.ds(0, n, stride=2), :] + t[pl.ds(1, n, stride=2), :]

    def window(h):
        return OWN - h, PLANES + 2 * h

    rows1 = NY // 2
    even = lax.broadcasted_iota(jnp.int32, (rows1, NX), 1) % 2 == 0

    def give(cycle, i):
        return remote(
            g.at[cycle, d], g.at[cycle, d], g_s.at[cycle, i], g_r.at[cycle, i],
            (b, lax.rem(d + i, domains)),
        )

    def take(cycle, i):
        origin = lax.rem(d + (domains - i), domains)
        return origin, remote(
            g.at[cycle, origin], g.at[cycle, origin], g_s.at[cycle, i], g_r.at[cycle, i], (b, origin)
        )

    def packed(v, source, at, to):
        a = pooled(v, source, 0, at, t0)
        a = a + pltpu.roll(a, NX - 1, 1)
        e = pooled(v, source, 0, to, t1)
        e = e + pltpu.roll(e, 1, 1)
        return 0.5 * jnp.where(even, a, e)

    def restrict_and_send(v, cycle):
        g[cycle, d] = packed(v, fx, OWN, OWN + 2)
        for i in range(1, domains):
            give(cycle, i).start()

    sibling = d + 1 - 2 * lax.rem(d, 2)
    chips = domains // 2

    def sum_up():
        return remote(share, share_outer, sum_s.at[0], sum_r.at[0], (inner, d))

    def sum_mid():
        return remote(share, share_inner, sum_s.at[1], sum_r.at[1], (inner, d))

    def sum_down(dev):
        return remote(shares.at[d], shares.at[d], sum_s.at[2], sum_r.at[2], (dev, d))

    def tell(i):
        dev = sibling if i == 0 else lax.rem(d + 2 * i, domains)
        return remote(shares.at[d], shares.at[d], share_s.at[i], share_r.at[i], (b, dev))

    def told(i):
        origin = sibling if i == 0 else lax.rem(d + (domains - 2 * i), domains)
        return remote(shares.at[origin], shares.at[origin], share_s.at[i], share_r.at[i], (b, origin))

    def hand_on(i):
        origin = lax.rem(d + (domains - 2 * i), domains)
        return remote(shares.at[origin], shares.at[origin], pass_s.at[i], pass_r.at[i], (b, sibling))

    def handed(i):
        origin = lax.rem(sibling + (domains - 2 * i), domains)
        return remote(shares.at[origin], shares.at[origin], pass_s.at[i], pass_r.at[i], (b, sibling))

    def make_share():
        first(va, vb, 0, *window(1))
        share[0] = packed(vb, va, OWN, OWN + 2)
        share[1] = packed(vb, va, OWN - 2, OWN + 4)

    def gather_share(at_centre):
        @pl.when(has_outer)
        def _():
            sum_up().wait_recv()
            share[...] = share[...] + share_outer[...]

        (sum_mid() if at_centre else sum_up()).start()

    def spread_share(at_centre):
        if at_centre:
            sum_mid().wait_recv()
            shares[d] = share[...] + share_inner[...]
        else:
            sum_down(inner).wait_recv()

        @pl.when(has_outer)
        def _():
            sum_down(outer).start()

        for i in range(chips):
            tell(i).start()

    order = list(range(EARLY)) + [None] + list(range(EARLY, CHUNKS))

    def gather_step(n, at_centre):
        if order[n] is None:
            gather_share(at_centre)
        else:
            gathered(order[n], at_centre)

    def spread_step(n, at_centre):
        if order[n] is None:
            spread_share(at_centre)
        else:
            spread(order[n], at_centre)

    def total_share(e, j):
        below = shares[jnp.maximum(e - 1, 0), 1] * jnp.where(e > 0, 1.0, 0.0)
        above = shares[jnp.minimum(e + 1, domains - 1), 1] * jnp.where(e < domains - 1, 1.0, 0.0)
        a = shares[e, 0] + jnp.where(even, pltpu.roll(below, NX - 1, 1), pltpu.roll(above, 1, 1))
        f1[1 + 2 * e, PAD:PAD + rows1, :] = jnp.where(even, a, pltpu.roll(a, 1, 1))
        f1[2 + 2 * e, PAD:PAD + rows1, :] = jnp.where(even, pltpu.roll(a, NX - 1, 1), a)

    def gathered_shares():
        told(0).wait_recv()
        for i in range(1, chips):
            handed(i).wait_recv()
        loop(0, domains, total_share, 2)

    def gathered_residuals():
        unpack(1, d)
        for i in range(1, domains):
            origin, copy = take(1, i)
            copy.wait_recv()
            unpack(1, origin)

    def unpack(cycle, origin):
        a = g[cycle, origin]
        f1[1 + 2 * origin, PAD:PAD + rows1, :] = jnp.where(even, a, pltpu.roll(a, 1, 1))
        f1[2 + 2 * origin, PAD:PAD + rows1, :] = jnp.where(even, pltpu.roll(a, NX - 1, 1), a)

    def widen(a, level):
        width = 1 << level
        lane = lax.broadcasted_iota(jnp.int32, a.shape, 1)
        low = (lane // width) % 2 == 0
        return 0.5 * (a + jnp.where(low, pltpu.roll(a, NX - width, 1), pltpu.roll(a, width, 1)))

    def add_rows(dst, p, value, n):
        for odd in range(2):
            at = (p, pl.ds(PAD + odd, n, stride=2), slice(None))
            dst[at] = dst[at] + value

    def coarse(arrive, near, between):
        arrive()
        first(f1, u1a, 1, 1, n1)

        def down1(q, j):
            f2[1 + q, PAD:PAD + NY // 4, :] = widen(pooled(u1a, f1, 1, 1 + 2 * q, spare[j]), 1)

        loop(0, n2, down1)
        between()
        first(f2, u2a, 2, 1, n2)
        rows3 = NY // 8

        def down2(q, j):
            f3[pl.ds(pl.multiple_of(q * rows3, 8), rows3), :] = widen(pooled(u2a, f2, 2, 1 + 2 * q, spare[j]), 2)

        loop(0, n3, down2)
        dot = functools.partial(
            jnp.dot, precision=lax.Precision.HIGHEST, preferred_element_type=jnp.float32
        )
        modes = dot(left[...], dot(f3[...], into[...])) * weight[...]
        f3[...] = dot(dot(left[...], modes), back[...])

        def back2(q, j):
            value = f3[pl.ds(pl.multiple_of(q * rows3, 8), rows3), :]
            add_rows(u2a, 1 + 2 * q, value, rows3)
            add_rows(u2a, 2 + 2 * q, value, rows3)

        loop(0, n3, back2)
        sweep(u2a, f2, u2b, 2, 1, n2)
        sweep(u2b, f2, u2a, 2, 1, n2)

        def back1(q, j):
            value = u2a[1 + q, PAD:PAD + NY // 4, :]
            add_rows(u1a, 1 + 2 * q, value, NY // 4)
            add_rows(u1a, 2 + 2 * q, value, NY // 4)

        loop(0, n2, back1)
        for extra, src, dst in ((1, u1a, u1b), (0, u1b, u1a)):
            count = min(n1, 2 + 2 * (near + extra))
            start = jnp.clip(2 * d - near - extra, 0, n1 - count)
            sweep(src, f1, dst, 1, start + 1, count)

    def correct(v, near):
        for j in range(-near, 2 + near):
            z = 2 * d + j
            w = 2 * j + OWN

            @pl.when(jnp.logical_and(z >= 0, z < n1))
            def _():
                value = u1a[z + 1, PAD:PAD + rows1, :]
                add_rows(v, w, value, rows1)
                add_rows(v, w + 1, value, rows1)

    @pl.when(jnp.logical_not(centre))
    def _():
        for n in range(EARLY):
            gather_step(n, False)

    make_share()

    @pl.when(centre)
    def _():
        for n in range(len(order) + LAG):
            if n < len(order):
                gather_step(n, True)
            if n >= LAG:
                spread_step(n - LAG, True)

    @pl.when(jnp.logical_not(centre))
    def _():
        for n in range(EARLY, len(order)):
            gather_step(n, False)
        for n in range(len(order)):
            spread_step(n, False)

    for i in range(1, chips):
        told(i).wait_recv()
        hand_on(i).start()

    def near_arrived():
        for c in range(CHUNKS):
            @pl.when(d < domains - 1)
            def _():
                near_down(c).wait_recv()

            @pl.when(d > 0)
            def _():
                near_up(c).wait_recv()

        for i in range(2):
            @pl.when(onward[i][4])
            def _():
                for h in range(HALVES):
                    onward_copy(i, h).start()

        for table in tables[1:]:
            table.wait()

    coarse(gathered_shares, 3, near_arrived)
    first(fx, vb, 0, *window(1))

    for i in range(4):
        @pl.when(far[i][4])
        def _():
            for h in range(HALVES):
                far_copy(i, h).wait_recv()

    first(fx, vb, 0, OWN - 5, 4)
    first(fx, vb, 0, OWN + PLANES + 1, 4)
    correct(vb, 3)
    sweep(vb, fx, va, 0, *window(4))
    sweep(va, fx, vb, 0, *window(3))

    sweep(vb, fx, va, 0, *window(2))
    sweep(va, fx, vc, 0, *window(1))
    restrict_and_send(vc, 1)

    def v_up():
        return remote(
            vc.at[pl.ds(OWN + 2, 2), pl.ds(PAD, NY), :], hv.at[0], hv_s.at[0], hv_r.at[0], (b, d + 1)
        )

    def v_down():
        return remote(
            vc.at[pl.ds(OWN, 2), pl.ds(PAD, NY), :], hv.at[1], hv_s.at[1], hv_r.at[1], (b, d - 1)
        )

    @pl.when(d < domains - 1)
    def _():
        v_up().start()

    @pl.when(d > 0)
    def _():
        v_down().start()

    coarse(gathered_residuals, 1, lambda: None)

    @pl.when(d < domains - 1)
    def _():
        v_up().wait_send()
        v_down().wait_recv()
        vc[OWN + 4:OWN + 6, PAD:PAD + NY, :] = hv[1]

    @pl.when(d > 0)
    def _():
        v_down().wait_send()
        v_up().wait_recv()
        vc[OWN - 2:OWN, PAD:PAD + NY, :] = hv[0]

    for c in range(CHUNKS):
        @pl.when(centre)
        def _():
            mid(c).wait_send()

        @pl.when(jnp.logical_not(centre))
        def _():
            up(c).wait_send()

    correct(vc, 1)
    sweep(vc, fx, va, 0, *window(1))
    for p in range(PLANES):
        for r0, rn in blocks(0):
            c, total = beside(va, OWN + p, r0, rn, 1)
            f = fx[OWN + p, PAD + r0:PAD + r0 + rn, :]
            acc[p, r0:r0 + rn, :] = KEEP * c + GAIN[0] * (f + total)
        result(p).start()
    for p in range(PLANES):
        result(p).wait()

    for c in range(CHUNKS):
        @pl.when(has_outer)
        def _():
            down(c, outer).wait_send()

        @pl.when(d < domains - 1)
        def _():
            near_up(c).wait_send()

        @pl.when(d > 0)
        def _():
            near_down(c).wait_send()

    for i in range(4):
        @pl.when(far[i][3])
        def _():
            for h in range(HALVES):
                far_copy(i, h).wait_send()

    for i in range(2):
        @pl.when(onward[i][4])
        def _():
            for h in range(HALVES):
                onward_copy(i, h).wait_send()

    for i in range(chips):
        tell(i).wait_send()
    for i in range(1, chips):
        hand_on(i).wait_send()
    for i in range(1, domains):
        give(1, i).wait_send()

    @pl.when(centre)
    def _():
        sum_mid().wait_send()

    @pl.when(jnp.logical_not(centre))
    def _():
        sum_up().wait_send()

    @pl.when(has_outer)
    def _():
        sum_down(outer).wait_send()


def potential_of(orbitals, occupations, bands, domains):
    n1, n2, n3 = 2 * domains, domains, domains // 2
    tables = coarse_basis(n3)
    f32 = jnp.float32
    count = orbitals.shape[0]
    pair = pltpu.VMEM((2, NY // 2, NX), f32)
    slab = pltpu.VMEM((PLANES, NY, NX), f32)
    fine = pltpu.VMEM((WINDOW, NY + 2 * PAD, NX), f32)
    level1 = pltpu.VMEM((n1 + 2, NY // 2 + 2 * PAD, NX), f32)
    level2 = pltpu.VMEM((n2 + 2, NY // 4 + 2 * PAD, NX), f32)
    chunk_sems = pltpu.SemaphoreType.DMA((CHUNKS,))
    near_sems = pltpu.SemaphoreType.DMA((2, CHUNKS))
    sum_sems = pltpu.SemaphoreType.DMA((3,))
    chip_sems = pltpu.SemaphoreType.DMA((domains // 2,))
    gather_sems = pltpu.SemaphoreType.DMA((2, domains))
    return pl.pallas_call(
        functools.partial(kernel, bands, domains, 0.5 * charge_scale / (count * bands)),
        out_shape=jax.ShapeDtypeStruct((PLANES, NY, NX), f32),
        in_specs=[pl.BlockSpec(memory_space=pl.ANY)] * 6,
        out_specs=pl.BlockSpec(memory_space=pl.ANY),
        scratch_shapes=[
            pltpu.SMEM(occupations.shape, jnp.int32),
            *[pltpu.VMEM(table.shape, f32) for table in tables],
            pltpu.VMEM(orbitals.shape, orbitals.dtype),
            pltpu.VMEM((NY * PLANES, NX), f32),
            pltpu.SemaphoreType.DMA((PLANES,)), pltpu.SemaphoreType.DMA((5,)), chunk_sems,
            slab, slab, slab, fine, fine, fine, fine,
            pltpu.VMEM((2, 2, NY, NX), f32),
            *[pltpu.VMEM((NY, NX), f32)] * 4,
            pltpu.VMEM((2, domains, NY // 2, NX), f32),
            pair, pair, pair, pltpu.VMEM((domains, 2, NY // 2, NX), f32),
            level1, level1, level1, level2, level2, level2,
            pltpu.VMEM((n3 * (NY // 8), NX), f32),
            chunk_sems, chunk_sems, chunk_sems, chunk_sems, chunk_sems, chunk_sems,
            near_sems, near_sems,
            pltpu.SemaphoreType.DMA((6, HALVES)), pltpu.SemaphoreType.DMA((4, HALVES)),
            pltpu.SemaphoreType.DMA((2,)), pltpu.SemaphoreType.DMA((2,)),
            gather_sems, gather_sems,
            sum_sems, sum_sems, chip_sems, chip_sems, chip_sems, chip_sems,
        ],
        compiler_params=pltpu.CompilerParams(
            collective_id=0, has_side_effects=True, vmem_limit_bytes=62_500_000
        ),
    )(occupations, orbitals, *[jnp.asarray(table) for table in tables])


def body(bands, domains, orbitals, occupations):
    values = orbitals.astype(jnp.float32)
    potential = potential_of(orbitals, occupations, bands, domains).reshape(orbitals.shape[1], NY * NX)
    applied = (potential[None] * values).astype(jnp.bfloat16)
    return (potential, applied)


def solution(mesh):
    return jax.shard_map(
        functools.partial(body, mesh.shape["band"], mesh.shape["dom"]),
        mesh=mesh,
        in_specs=(P("band", "dom", None), P("band")),
        out_specs=(P("dom", None), P("band", "dom", None)),
        check_vma=False,
    )
```

```python
import functools

import jax
import jax.numpy as jnp
import numpy as np
from jax import lax
from jax.experimental import pallas as pl
from jax.experimental.pallas import tpu as pltpu
from jax.sharding import PartitionSpec as P

NX = 128
NY = 192
COARSE = 48

screening = 0.02
relaxation = 0.8
charge_scale = 0.07

PLANES = 4
HALO = 6
OWN = HALO
WINDOW = PLANES + 2 * HALO
PAD = 8
CHUNKS = 8
LAG = 3
EARLY = 2
HALVES = 2
MOST = (4, 4, 8)
STEP = NY // CHUNKS
HALF = NY // HALVES
CENTRE = [6.0 + screening * 4.0**level for level in range(4)]
GAIN = [relaxation / centre for centre in CENTRE]
KEEP = 1.0 - relaxation


def sines(n):
    k = np.arange(1, n + 1)
    basis = np.sqrt(2.0 / (n + 1)) * np.sin(np.pi * np.outer(k, k) / (n + 1))
    return basis, 2.0 * np.cos(np.pi * k / (n + 1))


def coarse_basis(depth):
    rows, cols, copies = NY // 8, NX // 8, 8
    sz, ez = sines(depth)
    sy, ey = sines(rows)
    sx, ex = sines(cols)
    left = np.kron(sz, sy)
    into = np.zeros((NX, NX))
    into[::copies, :cols] = sx
    back = np.zeros((NX, NX))
    back[:cols] = np.repeat(sx, copies, axis=1)
    near = (ez[:, None] + ey[None, :]).reshape(-1, 1) + ex[None, :]
    rate = KEEP + GAIN[3] * near
    total = GAIN[3] * sum(rate**n for n in range(COARSE))
    weight = np.zeros((depth * rows, NX))
    weight[:, :cols] = total
    return [np.asarray(part, np.float32) for part in (left, into, back, weight)]


def kernel(
    bands, domains, scale,
    occupations, orbitals, left_in, into_in, back_in, weight_in,
    out,
    occ, left, into, back, weight, held, mixed, out_s, table_s, held_s,
    acc, from_outer, from_inner, fx, va, vb, vc, hv, t0, t1, t2, t3, g,
    share, share_outer, share_inner, shares,
    f1, u1a, u1b, f2, u2a, u2b, f3,
    up_s, up_r, mid_s, mid_r, down_s, down_r, near_s, near_r, far_s, far_r, hv_s, hv_r,
    sum_s, sum_r, share_s, share_r, pass_s, pass_r,
):
    b = lax.axis_index("band")
    d = lax.axis_index("dom")
    half = bands // 2
    lower = b < half
    inner = jnp.where(lower, b + 1, b - 1)
    outer = jnp.where(lower, b - 1, b + 1)
    has_outer = jnp.logical_and(b > 0, b < bands - 1)
    centre = jnp.logical_or(b == half - 1, b == half)
    n1, n2, n3 = 2 * domains, domains, domains // 2

    def remote(src, dst, ss, rs, dev):
        return pltpu.make_async_remote_copy(
            src_ref=src, dst_ref=dst, send_sem=ss, recv_sem=rs,
            device_id=dev, device_id_type=pl.DeviceIdType.MESH,
        )

    lanes = STEP * NX

    def fetch(c):
        at = (slice(None), slice(None), pl.ds(c * lanes, lanes))
        return pltpu.make_async_copy(orbitals.at[at], held.at[at], held_s.at[c])

    def result(p):
        rows = pl.ds(p * NY, NY)
        return pltpu.make_async_copy(mixed.at[rows], out.at[rows], out_s.at[p])

    tables = [
        pltpu.make_async_copy(src, dst, table_s.at[i])
        for i, (src, dst) in enumerate(
            ((occupations, occ), (left_in, left), (into_in, into), (back_in, back), (weight_in, weight))
        )
    ]
    tables[0].start()
    for c in range(CHUNKS):
        fetch(c).start()
    for table in tables[1:]:
        table.start()
    barrier = pltpu.get_barrier_semaphore()

    def greet(dev):
        pl.semaphore_signal(barrier, inc=1, device_id=dev, device_id_type=pl.DeviceIdType.MESH)

    for i in range(1, domains):
        greet((b, lax.rem(d + i, domains)))
    greet((inner, d))

    @pl.when(has_outer)
    def _():
        greet((outer, d))

    for ref in (fx, va, vb, vc, f1, u1a, u1b, f2, u2a, u2b):
        edge = jnp.zeros((ref.shape[0], PAD, NX), jnp.float32)
        ref[:, 0:PAD, :] = edge
        ref[:, ref.shape[1] - PAD:ref.shape[1], :] = edge

    def clear(ref, p):
        ref[p] = jnp.zeros(ref.shape[1:], jnp.float32)

    for ref in (f1, u1a, u1b, f2, u2a, u2b):
        clear(ref, 0)
        clear(ref, ref.shape[0] - 1)
    clear(vc, OWN - 2)
    clear(vc, OWN + 5)
    for p in (OWN - 2, OWN - 1, OWN + 4, OWN + 5):
        clear(va, p)
    for p in (OWN - 3, OWN - 2, OWN + 5, OWN + 6):
        clear(vb, p)
    for k in range(HALO):
        reach = -(-(HALO - k) // PLANES)

        @pl.when(d < reach)
        def _():
            clear(fx, k)

        @pl.when(d >= domains - reach)
        def _():
            clear(fx, WINDOW - 1 - k)

    def density(c):
        fetch(c).wait()
        total = None
        for i in range(orbitals.shape[0]):
            value = held[i, :, c * lanes:(c + 1) * lanes].astype(jnp.float32)
            term = (occ[i].astype(jnp.float32) * scale) * (value * value)
            total = term if total is None else total + term
        first_row = c * STEP * PLANES
        for y in range(STEP):
            at = first_row + y * PLANES
            mixed[at:at + PLANES, :] = total[:, y * NX:(y + 1) * NX]
        for p in range(PLANES):
            plane = mixed[pl.ds(first_row + p, STEP, stride=PLANES), :]
            acc[p, c * STEP:(c + 1) * STEP, :] = plane
            va[OWN + p, PAD + c * STEP:PAD + (c + 1) * STEP, :] = plane

    tables[0].wait()
    for c in range(CHUNKS):
        density(c)
    pl.semaphore_wait(barrier, domains + jnp.where(has_outer, 1, 0))

    def part(ref, c):
        return ref.at[:, pl.ds(c * STEP, STEP), :]

    def slab(c):
        return fx.at[pl.ds(OWN, PLANES), pl.ds(PAD + c * STEP, STEP), :]

    def up(c):
        return remote(part(acc, c), part(from_outer, c), up_s.at[c], up_r.at[c], (inner, d))

    def mid(c):
        return remote(part(acc, c), part(from_inner, c), mid_s.at[c], mid_r.at[c], (inner, d))

    def down(c, dev):
        return remote(slab(c), slab(c), down_s.at[c], down_r.at[c], (dev, d))

    def near_up(c):
        rows = pl.ds(PAD + c * STEP, STEP)
        return remote(
            fx.at[pl.ds(OWN + 2, 2), rows, :], fx.at[pl.ds(OWN - 2, 2), rows, :],
            near_s.at[0, c], near_r.at[0, c], (b, d + 1),
        )

    def near_down(c):
        rows = pl.ds(PAD + c * STEP, STEP)
        return remote(
            fx.at[pl.ds(OWN, 2), rows, :], fx.at[pl.ds(OWN + 4, 2), rows, :],
            near_s.at[1, c], near_r.at[1, c], (b, d - 1),
        )

    even_d = lax.rem(d, 2) == 0
    odd_d = lax.rem(d, 2) == 1
    far = [
        (OWN, OWN - 4, 1, d < domains - 1, d > 0),
        (OWN + 2, OWN + 6, -1, d > 0, d < domains - 1),
        (OWN + 2, OWN - 6, 2, jnp.logical_and(even_d, d < domains - 2), d > 1),
        (OWN, OWN + 8, -2, jnp.logical_and(odd_d, d > 1), d < domains - 2),
    ]

    def far_copy(i, h):
        at, to, offset, _, _ = far[i]
        rows = pl.ds(PAD + h * HALF, HALF)
        return remote(
            fx.at[pl.ds(at, 2), rows, :], fx.at[pl.ds(to, 2), rows, :],
            far_s.at[i, h], far_r.at[i, h], (b, d + offset),
        )

    onward = [
        (OWN - 2, OWN - 6, 1, 2, jnp.logical_and(even_d, d > 1)),
        (OWN + 4, OWN + 8, -1, 3, jnp.logical_and(odd_d, d < domains - 2)),
    ]

    def onward_copy(i, h):
        at, to, offset, slot, _ = onward[i]
        rows = pl.ds(PAD + h * HALF, HALF)
        return remote(
            fx.at[pl.ds(at, 2), rows, :], fx.at[pl.ds(to, 2), rows, :],
            far_s.at[slot + 2, h], far_r.at[slot, h], (b, d + offset),
        )

    def gathered(c, at_centre):
        rows = slice(c * STEP, (c + 1) * STEP)

        @pl.when(has_outer)
        def _():
            up(c).wait_recv()
            acc[:, rows, :] = acc[:, rows, :] + from_outer[:, rows, :]

        (mid(c) if at_centre else up(c)).start()

    def spread(c, at_centre):
        rows = slice(c * STEP, (c + 1) * STEP)
        if at_centre:
            mid(c).wait_recv()
            fx[OWN:OWN + PLANES, PAD + c * STEP:PAD + (c + 1) * STEP, :] = (
                acc[:, rows, :] + from_inner[:, rows, :]
            )
        else:
            down(c, inner).wait_recv()

        @pl.when(has_outer)
        def _():
            down(c, outer).start()

        @pl.when(d < domains - 1)
        def _():
            near_up(c).start()

        @pl.when(d > 0)
        def _():
            near_down(c).start()

        if (c + 1) % (CHUNKS // HALVES) == 0:
            for i in range(4):
                @pl.when(far[i][3])
                def _():
                    far_copy(i, c // (CHUNKS // HALVES)).start()

    def beside(src, p, r0, rn, width):
        c = src[p, PAD + r0:PAD + r0 + rn, :]
        lane = lax.broadcasted_iota(jnp.int32, (rn, NX), 1)
        total = src[p, PAD + r0 - 1:PAD + r0 + rn - 1, :] + src[p, PAD + r0 + 1:PAD + r0 + rn + 1, :]
        total = total + (src[p - 1, PAD + r0:PAD + r0 + rn, :] + src[p + 1, PAD + r0:PAD + r0 + rn, :])
        total = total + jnp.where(lane < width, 0.0, pltpu.roll(c, width, 1))
        total = total + jnp.where(lane >= NX - width, 0.0, pltpu.roll(c, NX - width, 1))
        return c, total

    def rows_of(level):
        return NY >> level

    def blocks(level):
        rn = 48 if rows_of(level) % 48 == 0 else rows_of(level)
        return [(r0, rn) for r0 in range(0, rows_of(level), rn)]

    def loop(lo, count, fn, most=4):
        group = max(n for n in range(1, most + 1) if count % n == 0)

        def step(i, carry):
            for j in range(group):
                fn(lo + i * group + j, j)
            return carry

        lax.fori_loop(0, count // group, step, 0)

    def gain(level, p):
        if level:
            return GAIN[level]
        z = PLANES * d - OWN + p
        inside = jnp.logical_and(z >= 0, z < PLANES * domains)
        return jnp.where(inside, jnp.float32(GAIN[0]), jnp.float32(0.0))

    def first(src, dst, level, lo, count):
        def plane(p, j):
            k = gain(level, p)
            for r0, rn in blocks(level):
                c, total = beside(src, p, r0, rn, 1 << level)
                dst[p, PAD + r0:PAD + r0 + rn, :] = (GAIN[level] * (1.0 + KEEP)) * c + (k * GAIN[level]) * total

        loop(lo, count, plane, MOST[level])

    def sweep(src, source, dst, level, lo, count):
        def plane(p, j):
            k = gain(level, p)
            for r0, rn in blocks(level):
                c, total = beside(src, p, r0, rn, 1 << level)
                f = source[p, PAD + r0:PAD + r0 + rn, :]
                dst[p, PAD + r0:PAD + r0 + rn, :] = KEEP * c + k * (f + total)

        loop(lo, count, plane, MOST[level])

    def residual(v, source, level, p, r0, rn):
        c, total = beside(v, p, r0, rn, 1 << level)
        return source[p, PAD + r0:PAD + r0 + rn, :] + total - CENTRE[level] * c

    spare = (t0, t1, t2, t3)

    def pooled(v, source, level, p, t):
        for r0, rn in blocks(level):
            t[r0:r0 + rn, :] = residual(v, source, level, p, r0, rn) + residual(v, source, level, p + 1, r0, rn)
        n = rows_of(level) // 2
        return t[pl.ds(0, n, stride=2), :] + t[pl.ds(1, n, stride=2), :]

    def window(h):
        return OWN - h, PLANES + 2 * h

    rows1 = NY // 2
    even = lax.broadcasted_iota(jnp.int32, (rows1, NX), 1) % 2 == 0

    def packed(v, source, at, to):
        a = pooled(v, source, 0, at, t0)
        a = a + pltpu.roll(a, NX - 1, 1)
        e = pooled(v, source, 0, to, t1)
        e = e + pltpu.roll(e, 1, 1)
        return 0.5 * jnp.where(even, a, e)

    def restrict_and_send(v, cycle):
        g[cycle, d] = packed(v, fx, OWN, OWN + 2)
        for i in range(1, chips):
            tell(i, cycle).start()
        tell(0, cycle).start()

    sibling = d + 1 - 2 * lax.rem(d, 2)
    chips = domains // 2

    def sum_up():
        return remote(share, share_outer, sum_s.at[0], sum_r.at[0], (inner, d))

    def sum_mid():
        return remote(share, share_inner, sum_s.at[1], sum_r.at[1], (inner, d))

    def sum_down(dev):
        return remote(shares.at[d], shares.at[d], sum_s.at[2], sum_r.at[2], (dev, d))

    def block(cycle, origin):
        return g.at[1, origin] if cycle else shares.at[origin]

    def tell(i, cycle):
        dev = sibling if i == 0 else lax.rem(d + 2 * i, domains)
        src = block(cycle, d)
        return remote(src, src, share_s.at[cycle, i], share_r.at[cycle, i], (b, dev))

    def origin_of(i, near):
        return sibling if i == 0 else lax.rem(near + (domains - 2 * i), domains)

    def told(i, cycle):
        origin = origin_of(i, d)
        src = block(cycle, origin)
        return remote(src, src, share_s.at[cycle, i], share_r.at[cycle, i], (b, origin))

    def hand_on(i, cycle):
        src = block(cycle, origin_of(i, d))
        return remote(src, src, pass_s.at[cycle, i], pass_r.at[cycle, i], (b, sibling))

    def handed(i, cycle):
        src = block(cycle, origin_of(i, sibling))
        return remote(src, src, pass_s.at[cycle, i], pass_r.at[cycle, i], (b, sibling))

    def make_share():
        first(va, vb, 0, *window(1))
        share[0] = packed(vb, va, OWN, OWN + 2)
        share[1] = packed(vb, va, OWN - 2, OWN + 4)

    def gather_share(at_centre):
        @pl.when(has_outer)
        def _():
            sum_up().wait_recv()
            share[...] = share[...] + share_outer[...]

        (sum_mid() if at_centre else sum_up()).start()

    def spread_share(at_centre):
        if at_centre:
            sum_mid().wait_recv()
            shares[d] = share[...] + share_inner[...]
        else:
            sum_down(inner).wait_recv()

        @pl.when(has_outer)
        def _():
            sum_down(outer).start()

        for i in range(chips):
            tell(i, 0).start()

    order = list(range(EARLY)) + [None] + list(range(EARLY, CHUNKS))

    def gather_step(n, at_centre):
        if order[n] is None:
            gather_share(at_centre)
        else:
            gathered(order[n], at_centre)

    def spread_step(n, at_centre):
        if order[n] is None:
            spread_share(at_centre)
        else:
            spread(order[n], at_centre)

    def total_share(e, j):
        below = shares[jnp.maximum(e - 1, 0), 1] * jnp.where(e > 0, 1.0, 0.0)
        above = shares[jnp.minimum(e + 1, domains - 1), 1] * jnp.where(e < domains - 1, 1.0, 0.0)
        a = shares[e, 0] + jnp.where(even, pltpu.roll(below, NX - 1, 1), pltpu.roll(above, 1, 1))
        f1[1 + 2 * e, PAD:PAD + rows1, :] = jnp.where(even, a, pltpu.roll(a, 1, 1))
        f1[2 + 2 * e, PAD:PAD + rows1, :] = jnp.where(even, pltpu.roll(a, NX - 1, 1), a)

    def gathered_shares():
        told(0, 0).wait_recv()
        for i in range(1, chips):
            handed(i, 0).wait_recv()
        loop(0, domains, total_share, 2)

    def gathered_residuals():
        for i in range(1, chips):
            told(i, 1).wait_recv()
            hand_on(i, 1).start()
        unpack(1, d)
        for i in range(1, chips):
            unpack(1, origin_of(i, d))
        told(0, 1).wait_recv()
        unpack(1, sibling)
        for i in range(1, chips):
            handed(i, 1).wait_recv()
            unpack(1, origin_of(i, sibling))

    def unpack(cycle, origin):
        a = g[cycle, origin]
        f1[1 + 2 * origin, PAD:PAD + rows1, :] = jnp.where(even, a, pltpu.roll(a, 1, 1))
        f1[2 + 2 * origin, PAD:PAD + rows1, :] = jnp.where(even, pltpu.roll(a, NX - 1, 1), a)

    def widen(a, level):
        width = 1 << level
        lane = lax.broadcasted_iota(jnp.int32, a.shape, 1)
        low = (lane // width) % 2 == 0
        return 0.5 * (a + jnp.where(low, pltpu.roll(a, NX - width, 1), pltpu.roll(a, width, 1)))

    def add_rows(dst, p, value, n):
        for odd in range(2):
            at = (p, pl.ds(PAD + odd, n, stride=2), slice(None))
            dst[at] = dst[at] + value

    def coarse(arrive, near, between):
        arrive()
        first(f1, u1a, 1, 1, n1)

        def down1(q, j):
            f2[1 + q, PAD:PAD + NY // 4, :] = widen(pooled(u1a, f1, 1, 1 + 2 * q, spare[j]), 1)

        loop(0, n2, down1)
        between()
        first(f2, u2a, 2, 1, n2)
        rows3 = NY // 8

        def down2(q, j):
            f3[pl.ds(pl.multiple_of(q * rows3, 8), rows3), :] = widen(pooled(u2a, f2, 2, 1 + 2 * q, spare[j]), 2)

        loop(0, n3, down2)
        dot = functools.partial(
            jnp.dot, precision=lax.Precision.HIGHEST, preferred_element_type=jnp.float32
        )
        modes = dot(left[...], dot(f3[...], into[...])) * weight[...]
        f3[...] = dot(dot(left[...], modes), back[...])

        def back2(q, j):
            value = f3[pl.ds(pl.multiple_of(q * rows3, 8), rows3), :]
            add_rows(u2a, 1 + 2 * q, value, rows3)
            add_rows(u2a, 2 + 2 * q, value, rows3)

        loop(0, n3, back2)
        sweep(u2a, f2, u2b, 2, 1, n2)
        sweep(u2b, f2, u2a, 2, 1, n2)

        def back1(q, j):
            value = u2a[1 + q, PAD:PAD + NY // 4, :]
            add_rows(u1a, 1 + 2 * q, value, NY // 4)
            add_rows(u1a, 2 + 2 * q, value, NY // 4)

        loop(0, n2, back1)
        for extra, src, dst in ((1, u1a, u1b), (0, u1b, u1a)):
            count = min(n1, 2 + 2 * (near + extra))
            start = jnp.clip(2 * d - near - extra, 0, n1 - count)
            sweep(src, f1, dst, 1, start + 1, count)

    def correct(v, near):
        for j in range(-near, 2 + near):
            z = 2 * d + j
            w = 2 * j + OWN

            @pl.when(jnp.logical_and(z >= 0, z < n1))
            def _():
                value = u1a[z + 1, PAD:PAD + rows1, :]
                add_rows(v, w, value, rows1)
                add_rows(v, w + 1, value, rows1)

    @pl.when(jnp.logical_not(centre))
    def _():
        for n in range(EARLY):
            gather_step(n, False)

    make_share()

    @pl.when(centre)
    def _():
        for n in range(len(order) + LAG):
            if n < len(order):
                gather_step(n, True)
            if n >= LAG:
                spread_step(n - LAG, True)

    @pl.when(jnp.logical_not(centre))
    def _():
        for n in range(EARLY, len(order)):
            gather_step(n, False)
        for n in range(len(order)):
            spread_step(n, False)

    for i in range(1, chips):
        told(i, 0).wait_recv()
        hand_on(i, 0).start()

    def near_arrived():
        for c in range(CHUNKS):
            @pl.when(d < domains - 1)
            def _():
                near_down(c).wait_recv()

            @pl.when(d > 0)
            def _():
                near_up(c).wait_recv()

        for i in range(2):
            @pl.when(onward[i][4])
            def _():
                for h in range(HALVES):
                    onward_copy(i, h).start()

        for table in tables[1:]:
            table.wait()

    coarse(gathered_shares, 3, near_arrived)
    first(fx, vb, 0, *window(1))

    for i in range(4):
        @pl.when(far[i][4])
        def _():
            for h in range(HALVES):
                far_copy(i, h).wait_recv()

    first(fx, vb, 0, OWN - 5, 4)
    first(fx, vb, 0, OWN + PLANES + 1, 4)
    correct(vb, 3)
    sweep(vb, fx, va, 0, *window(4))
    sweep(va, fx, vb, 0, *window(3))

    sweep(vb, fx, va, 0, *window(2))
    sweep(va, fx, vc, 0, *window(1))
    restrict_and_send(vc, 1)

    def v_up():
        return remote(
            vc.at[pl.ds(OWN + 2, 2), pl.ds(PAD, NY), :], hv.at[0], hv_s.at[0], hv_r.at[0], (b, d + 1)
        )

    def v_down():
        return remote(
            vc.at[pl.ds(OWN, 2), pl.ds(PAD, NY), :], hv.at[1], hv_s.at[1], hv_r.at[1], (b, d - 1)
        )

    @pl.when(d < domains - 1)
    def _():
        v_up().start()

    @pl.when(d > 0)
    def _():
        v_down().start()

    coarse(gathered_residuals, 1, lambda: None)

    @pl.when(d < domains - 1)
    def _():
        v_up().wait_send()
        v_down().wait_recv()
        vc[OWN + 4:OWN + 6, PAD:PAD + NY, :] = hv[1]

    @pl.when(d > 0)
    def _():
        v_down().wait_send()
        v_up().wait_recv()
        vc[OWN - 2:OWN, PAD:PAD + NY, :] = hv[0]

    for c in range(CHUNKS):
        @pl.when(centre)
        def _():
            mid(c).wait_send()

        @pl.when(jnp.logical_not(centre))
        def _():
            up(c).wait_send()

    correct(vc, 1)
    sweep(vc, fx, va, 0, *window(1))
    for k, (r0, rn) in enumerate(blocks(0)):
        for p in range(PLANES):
            c, total = beside(va, OWN + p, r0, rn, 1)
            f = fx[OWN + p, PAD + r0:PAD + r0 + rn, :]
            mixed[pl.ds(r0 * PLANES + p, rn, stride=PLANES), :] = KEEP * c + GAIN[0] * (f + total)
        result(k).start()
    for k in range(4):
        result(k).wait()

    for c in range(CHUNKS):
        @pl.when(has_outer)
        def _():
            down(c, outer).wait_send()

        @pl.when(d < domains - 1)
        def _():
            near_up(c).wait_send()

        @pl.when(d > 0)
        def _():
            near_down(c).wait_send()

    for i in range(4):
        @pl.when(far[i][3])
        def _():
            for h in range(HALVES):
                far_copy(i, h).wait_send()

    for i in range(2):
        @pl.when(onward[i][4])
        def _():
            for h in range(HALVES):
                onward_copy(i, h).wait_send()

    for cycle in range(2):
        for i in range(chips):
            tell(i, cycle).wait_send()
        for i in range(1, chips):
            hand_on(i, cycle).wait_send()

    @pl.when(centre)
    def _():
        sum_mid().wait_send()

    @pl.when(jnp.logical_not(centre))
    def _():
        sum_up().wait_send()

    @pl.when(has_outer)
    def _():
        sum_down(outer).wait_send()


def potential_of(orbitals, occupations, bands, domains):
    n1, n2, n3 = 2 * domains, domains, domains // 2
    tables = coarse_basis(n3)
    f32 = jnp.float32
    count = orbitals.shape[0]
    pair = pltpu.VMEM((2, NY // 2, NX), f32)
    slab = pltpu.VMEM((PLANES, NY, NX), f32)
    fine = pltpu.VMEM((WINDOW, NY + 2 * PAD, NX), f32)
    level1 = pltpu.VMEM((n1 + 2, NY // 2 + 2 * PAD, NX), f32)
    level2 = pltpu.VMEM((n2 + 2, NY // 4 + 2 * PAD, NX), f32)
    chunk_sems = pltpu.SemaphoreType.DMA((CHUNKS,))
    near_sems = pltpu.SemaphoreType.DMA((2, CHUNKS))
    sum_sems = pltpu.SemaphoreType.DMA((3,))
    chip_sems = pltpu.SemaphoreType.DMA((2, domains // 2))
    return pl.pallas_call(
        functools.partial(kernel, bands, domains, 0.5 * charge_scale / (count * bands)),
        out_shape=jax.ShapeDtypeStruct((NY * PLANES, NX), f32),
        in_specs=[pl.BlockSpec(memory_space=pl.ANY)] * 6,
        out_specs=pl.BlockSpec(memory_space=pl.ANY),
        scratch_shapes=[
            pltpu.SMEM(occupations.shape, jnp.int32),
            *[pltpu.VMEM(table.shape, f32) for table in tables],
            pltpu.VMEM(orbitals.shape, orbitals.dtype),
            pltpu.VMEM((NY * PLANES, NX), f32),
            pltpu.SemaphoreType.DMA((PLANES,)), pltpu.SemaphoreType.DMA((5,)), chunk_sems,
            slab, slab, slab, fine, fine, fine, fine,
            pltpu.VMEM((2, 2, NY, NX), f32),
            *[pltpu.VMEM((NY, NX), f32)] * 4,
            pltpu.VMEM((2, domains, NY // 2, NX), f32),
            pair, pair, pair, pltpu.VMEM((domains, 2, NY // 2, NX), f32),
            level1, level1, level1, level2, level2, level2,
            pltpu.VMEM((n3 * (NY // 8), NX), f32),
            chunk_sems, chunk_sems, chunk_sems, chunk_sems, chunk_sems, chunk_sems,
            near_sems, near_sems,
            pltpu.SemaphoreType.DMA((6, HALVES)), pltpu.SemaphoreType.DMA((4, HALVES)),
            pltpu.SemaphoreType.DMA((2,)), pltpu.SemaphoreType.DMA((2,)),
            sum_sems, sum_sems, chip_sems, chip_sems, chip_sems, chip_sems,
        ],
        compiler_params=pltpu.CompilerParams(
            collective_id=0, has_side_effects=True, vmem_limit_bytes=62_500_000
        ),
    )(occupations, orbitals, *[jnp.asarray(table) for table in tables])


def apply(mixed_in, orbitals, potential, applied, mixed, flat, held, in_s, orb_s, flat_s, held_s):
    rows, lanes = STEP * PLANES, STEP * NX

    def fetch(c):
        at = pl.ds(c * rows, rows)
        return pltpu.make_async_copy(mixed_in.at[at], mixed.at[at], in_s.at[c])

    def read(c):
        at = (slice(None), slice(None), pl.ds(c * lanes, lanes))
        return pltpu.make_async_copy(orbitals.at[at], held.at[at], orb_s.at[c])

    def keep(c):
        at = (slice(None), pl.ds(c * lanes, lanes))
        return pltpu.make_async_copy(flat.at[at], potential.at[at], flat_s.at[c])

    def store(c):
        at = (slice(None), slice(None), pl.ds(c * lanes, lanes))
        return pltpu.make_async_copy(held.at[at], applied.at[at], held_s.at[c])

    for c in range(CHUNKS):
        fetch(c).start()
        read(c).start()
    for c in range(CHUNKS):
        fetch(c).wait()
        for y in range(c * STEP, (c + 1) * STEP):
            flat[:, y * NX:(y + 1) * NX] = mixed[y * PLANES:(y + 1) * PLANES, :]
        keep(c).start()
        value = flat[:, c * lanes:(c + 1) * lanes]
        read(c).wait()
        for i in range(orbitals.shape[0]):
            psi = held[i, :, c * lanes:(c + 1) * lanes].astype(jnp.float32)
            held[i, :, c * lanes:(c + 1) * lanes] = (value * psi).astype(held.dtype)
        store(c).start()
    for c in range(CHUNKS):
        keep(c).wait()
        store(c).wait()


def applied_of(mixed, orbitals):
    flat = (PLANES, NY * NX)
    sems = pltpu.SemaphoreType.DMA((CHUNKS,))
    anywhere = pl.BlockSpec(memory_space=pl.ANY)
    return pl.pallas_call(
        apply,
        out_shape=(
            jax.ShapeDtypeStruct(flat, jnp.float32),
            jax.ShapeDtypeStruct(orbitals.shape, orbitals.dtype),
        ),
        in_specs=[anywhere, anywhere],
        out_specs=(anywhere, anywhere),
        scratch_shapes=[
            pltpu.VMEM((NY * PLANES, NX), jnp.float32),
            pltpu.VMEM(flat, jnp.float32),
            pltpu.VMEM(orbitals.shape, orbitals.dtype),
            sems, sems, sems, sems,
        ],
        compiler_params=pltpu.CompilerParams(vmem_limit_bytes=62_500_000),
    )(mixed, orbitals)


def body(bands, domains, orbitals, occupations):
    return applied_of(potential_of(orbitals, occupations, bands, domains), orbitals)


def solution(mesh):
    return jax.shard_map(
        functools.partial(body, mesh.shape["band"], mesh.shape["dom"]),
        mesh=mesh,
        in_specs=(P("band", "dom", None), P("band")),
        out_specs=(P("dom", None), P("band", "dom", None)),
        check_vma=False,
    )
```

```python
import functools

import jax
import jax.numpy as jnp
import numpy as np
from jax import lax
from jax.experimental import pallas as pl
from jax.experimental.pallas import tpu as pltpu
from jax.sharding import PartitionSpec as P

NX = 128
NY = 192
COARSE = 48

screening = 0.02
relaxation = 0.8
charge_scale = 0.07

PLANES = 4
HALO = 6
OWN = HALO
WINDOW = PLANES + 2 * HALO
PAD = 8
CHUNKS = 8
LAG = 3
EARLY = 2
ROOM = 8192
HALVES = 2
MOST = (4, 4, 8)
STEP = NY // CHUNKS
HALF = NY // HALVES
CENTRE = [6.0 + screening * 4.0**level for level in range(4)]
GAIN = [relaxation / centre for centre in CENTRE]
KEEP = 1.0 - relaxation


def sines(n):
    k = np.arange(1, n + 1)
    basis = np.sqrt(2.0 / (n + 1)) * np.sin(np.pi * np.outer(k, k) / (n + 1))
    return basis, 2.0 * np.cos(np.pi * k / (n + 1))


def coarse_basis(depth):
    rows, cols, copies = NY // 8, NX // 8, 8
    sz, ez = sines(depth)
    sy, ey = sines(rows)
    sx, ex = sines(cols)
    left = np.kron(sz, sy)
    into = np.zeros((NX, NX))
    into[::copies, :cols] = sx
    back = np.zeros((NX, NX))
    back[:cols] = np.repeat(sx, copies, axis=1)
    near = (ez[:, None] + ey[None, :]).reshape(-1, 1) + ex[None, :]
    rate = KEEP + GAIN[3] * near
    total = GAIN[3] * sum(rate**n for n in range(COARSE))
    weight = np.zeros((depth * rows, NX))
    weight[:, :cols] = total
    return [np.asarray(part, np.float32) for part in (left, into, back, weight)]


def kernel(
    bands, domains, scale,
    occupations, orbitals, left_in, into_in, back_in, weight_in,
    out,
    occ, left, into, back, weight, held, mixed, out_s, table_s, held_s,
    acc, from_outer, from_inner, fx, va, vb, vc, hv, t0, t1, t2, t3, g,
    share, share_outer, share_inner, shares,
    f1, u1a, u1b, f2, u2a, u2b, f3,
    up_s, up_r, mid_s, mid_r, down_s, down_r, near_s, near_r, far_s, far_r, hv_s, hv_r,
    sum_s, sum_r, share_s, share_r, pass_s, pass_r,
):
    b = lax.axis_index("band")
    d = lax.axis_index("dom")
    half = bands // 2
    lower = b < half
    inner = jnp.where(lower, b + 1, b - 1)
    outer = jnp.where(lower, b - 1, b + 1)
    has_outer = jnp.logical_and(b > 0, b < bands - 1)
    centre = jnp.logical_or(b == half - 1, b == half)
    n1, n2, n3 = 2 * domains, domains, domains // 2

    def remote(src, dst, ss, rs, dev):
        return pltpu.make_async_remote_copy(
            src_ref=src, dst_ref=dst, send_sem=ss, recv_sem=rs,
            device_id=dev, device_id_type=pl.DeviceIdType.MESH,
        )

    lines = STEP * PLANES

    def fetch(c):
        at = (slice(None), pl.ds(c * lines, lines), slice(None))
        return pltpu.make_async_copy(orbitals.at[at], held.at[at], held_s.at[c])

    def result(p):
        r0, rn = blocks(0)[p]
        rows = pl.ds(r0 * PLANES, rn * PLANES)
        return pltpu.make_async_copy(mixed.at[rows], out.at[rows], out_s.at[p])

    tables = [
        pltpu.make_async_copy(src, dst, table_s.at[i])
        for i, (src, dst) in enumerate(
            ((occupations, occ), (left_in, left), (into_in, into), (back_in, back), (weight_in, weight))
        )
    ]
    tables[0].start()
    for c in range(CHUNKS):
        fetch(c).start()
    for table in tables[1:]:
        table.start()
    barrier = pltpu.get_barrier_semaphore()

    def greet(dev):
        pl.semaphore_signal(barrier, inc=1, device_id=dev, device_id_type=pl.DeviceIdType.MESH)

    for i in range(1, domains):
        greet((b, lax.rem(d + i, domains)))
    greet((inner, d))

    @pl.when(has_outer)
    def _():
        greet((outer, d))

    for ref in (fx, va, vb, vc, f1, u1a, u1b, f2, u2a, u2b):
        edge = jnp.zeros((ref.shape[0], PAD, NX), jnp.float32)
        ref[:, 0:PAD, :] = edge
        ref[:, ref.shape[1] - PAD:ref.shape[1], :] = edge

    def clear(ref, p):
        ref[p] = jnp.zeros(ref.shape[1:], jnp.float32)

    for ref in (f1, u1a, u1b, f2, u2a, u2b):
        clear(ref, 0)
        clear(ref, ref.shape[0] - 1)
    clear(vc, OWN - 2)
    clear(vc, OWN + 5)
    for p in (OWN - 2, OWN - 1, OWN + 4, OWN + 5):
        clear(va, p)
    for p in (OWN - 3, OWN - 2, OWN + 5, OWN + 6):
        clear(vb, p)
    for k in range(HALO):
        reach = -(-(HALO - k) // PLANES)

        @pl.when(d < reach)
        def _():
            clear(fx, k)

        @pl.when(d >= domains - reach)
        def _():
            clear(fx, WINDOW - 1 - k)

    def density(c):
        fetch(c).wait()
        first_row = c * lines
        total = None
        for i in range(orbitals.shape[0]):
            value = held[i, first_row:first_row + lines, :].astype(jnp.float32)
            term = (occ[i].astype(jnp.float32) * scale) * (value * value)
            total = term if total is None else total + term
        mixed[first_row:first_row + lines, :] = total
        for p in range(PLANES):
            plane = mixed[pl.ds(first_row + p, STEP, stride=PLANES), :]
            acc[p, c * STEP:(c + 1) * STEP, :] = plane
            va[OWN + p, PAD + c * STEP:PAD + (c + 1) * STEP, :] = plane

    tables[0].wait()
    for c in range(EARLY):
        density(c)
    pl.semaphore_wait(barrier, domains + jnp.where(has_outer, 1, 0))

    def part(ref, c):
        return ref.at[:, pl.ds(c * STEP, STEP), :]

    def slab(c):
        return fx.at[pl.ds(OWN, PLANES), pl.ds(PAD + c * STEP, STEP), :]

    def up(c):
        return remote(part(acc, c), part(from_outer, c), up_s.at[c], up_r.at[c], (inner, d))

    def mid(c):
        return remote(part(acc, c), part(from_inner, c), mid_s.at[c], mid_r.at[c], (inner, d))

    def down(c, dev):
        return remote(slab(c), slab(c), down_s.at[c], down_r.at[c], (dev, d))

    def near_up(c):
        rows = pl.ds(PAD + c * STEP, STEP)
        return remote(
            fx.at[pl.ds(OWN + 2, 2), rows, :], fx.at[pl.ds(OWN - 2, 2), rows, :],
            near_s.at[0, c], near_r.at[0, c], (b, d + 1),
        )

    def near_down(c):
        rows = pl.ds(PAD + c * STEP, STEP)
        return remote(
            fx.at[pl.ds(OWN, 2), rows, :], fx.at[pl.ds(OWN + 4, 2), rows, :],
            near_s.at[1, c], near_r.at[1, c], (b, d - 1),
        )

    even_d = lax.rem(d, 2) == 0
    odd_d = lax.rem(d, 2) == 1
    far = [
        (OWN, OWN - 4, 1, d < domains - 1, d > 0),
        (OWN + 2, OWN + 6, -1, d > 0, d < domains - 1),
        (OWN + 2, OWN - 6, 2, jnp.logical_and(even_d, d < domains - 2), d > 1),
        (OWN, OWN + 8, -2, jnp.logical_and(odd_d, d > 1), d < domains - 2),
    ]

    def far_copy(i, h):
        at, to, offset, _, _ = far[i]
        rows = pl.ds(PAD + h * HALF, HALF)
        return remote(
            fx.at[pl.ds(at, 2), rows, :], fx.at[pl.ds(to, 2), rows, :],
            far_s.at[i, h], far_r.at[i, h], (b, d + offset),
        )

    onward = [
        (OWN - 2, OWN - 6, 1, 2, jnp.logical_and(even_d, d > 1)),
        (OWN + 4, OWN + 8, -1, 3, jnp.logical_and(odd_d, d < domains - 2)),
    ]

    def onward_copy(i, h):
        at, to, offset, slot, _ = onward[i]
        rows = pl.ds(PAD + h * HALF, HALF)
        return remote(
            fx.at[pl.ds(at, 2), rows, :], fx.at[pl.ds(to, 2), rows, :],
            far_s.at[slot + 2, h], far_r.at[slot, h], (b, d + offset),
        )

    def gathered(c, at_centre):
        rows = slice(c * STEP, (c + 1) * STEP)

        @pl.when(has_outer)
        def _():
            up(c).wait_recv()
            acc[:, rows, :] = acc[:, rows, :] + from_outer[:, rows, :]

        (mid(c) if at_centre else up(c)).start()

    def spread(c, at_centre):
        rows = slice(c * STEP, (c + 1) * STEP)
        if at_centre:
            mid(c).wait_recv()
            fx[OWN:OWN + PLANES, PAD + c * STEP:PAD + (c + 1) * STEP, :] = (
                acc[:, rows, :] + from_inner[:, rows, :]
            )
        else:
            down(c, inner).wait_recv()

        @pl.when(has_outer)
        def _():
            down(c, outer).start()

        @pl.when(d < domains - 1)
        def _():
            near_up(c).start()

        @pl.when(d > 0)
        def _():
            near_down(c).start()

        if (c + 1) % (CHUNKS // HALVES) == 0:
            for i in range(4):
                @pl.when(far[i][3])
                def _():
                    far_copy(i, c // (CHUNKS // HALVES)).start()

    def beside(src, p, r0, rn, width):
        c = src[p, PAD + r0:PAD + r0 + rn, :]
        lane = lax.broadcasted_iota(jnp.int32, (rn, NX), 1)
        total = src[p, PAD + r0 - 1:PAD + r0 + rn - 1, :] + src[p, PAD + r0 + 1:PAD + r0 + rn + 1, :]
        total = total + (src[p - 1, PAD + r0:PAD + r0 + rn, :] + src[p + 1, PAD + r0:PAD + r0 + rn, :])
        total = total + jnp.where(lane < width, 0.0, pltpu.roll(c, width, 1))
        total = total + jnp.where(lane >= NX - width, 0.0, pltpu.roll(c, NX - width, 1))
        return c, total

    def rows_of(level):
        return NY >> level

    def blocks(level):
        rn = 48 if rows_of(level) % 48 == 0 else rows_of(level)
        return [(r0, rn) for r0 in range(0, rows_of(level), rn)]

    def loop(lo, count, fn, most=4):
        group = max(n for n in range(1, most + 1) if count % n == 0)

        def step(i, carry):
            for j in range(group):
                fn(lo + i * group + j, j)
            return carry

        lax.fori_loop(0, count // group, step, 0)

    def gain(level, p):
        if level:
            return GAIN[level]
        z = PLANES * d - OWN + p
        inside = jnp.logical_and(z >= 0, z < PLANES * domains)
        return jnp.where(inside, jnp.float32(GAIN[0]), jnp.float32(0.0))

    def first(src, dst, level, lo, count):
        def plane(p, j):
            k = gain(level, p)
            for r0, rn in blocks(level):
                c, total = beside(src, p, r0, rn, 1 << level)
                dst[p, PAD + r0:PAD + r0 + rn, :] = (GAIN[level] * (1.0 + KEEP)) * c + (k * GAIN[level]) * total

        loop(lo, count, plane, MOST[level])

    def sweep(src, source, dst, level, lo, count):
        def plane(p, j):
            k = gain(level, p)
            for r0, rn in blocks(level):
                c, total = beside(src, p, r0, rn, 1 << level)
                f = source[p, PAD + r0:PAD + r0 + rn, :]
                dst[p, PAD + r0:PAD + r0 + rn, :] = KEEP * c + k * (f + total)

        loop(lo, count, plane, MOST[level])

    def residual(v, source, level, p, r0, rn):
        c, total = beside(v, p, r0, rn, 1 << level)
        return source[p, PAD + r0:PAD + r0 + rn, :] + total - CENTRE[level] * c

    spare = (t0, t1, t2, t3)

    def pooled(v, source, level, p, t):
        for r0, rn in blocks(level):
            t[r0:r0 + rn, :] = residual(v, source, level, p, r0, rn) + residual(v, source, level, p + 1, r0, rn)
        n = rows_of(level) // 2
        return t[pl.ds(0, n, stride=2), :] + t[pl.ds(1, n, stride=2), :]

    def window(h):
        return OWN - h, PLANES + 2 * h

    rows1 = NY // 2
    even = lax.broadcasted_iota(jnp.int32, (rows1, NX), 1) % 2 == 0

    def packed(v, source, at, to):
        a = pooled(v, source, 0, at, t0)
        a = a + pltpu.roll(a, NX - 1, 1)
        e = pooled(v, source, 0, to, t1)
        e = e + pltpu.roll(e, 1, 1)
        return 0.5 * jnp.where(even, a, e)

    def restrict_and_send(v, cycle):
        g[cycle, d] = packed(v, fx, OWN, OWN + 2)
        for i in range(1, chips):
            tell(i, cycle).start()
        tell(0, cycle).start()

    sibling = d + 1 - 2 * lax.rem(d, 2)
    chips = domains // 2

    def sum_up():
        return remote(share, share_outer, sum_s.at[0], sum_r.at[0], (inner, d))

    def sum_mid():
        return remote(share, share_inner, sum_s.at[1], sum_r.at[1], (inner, d))

    def sum_down(dev):
        return remote(shares.at[d], shares.at[d], sum_s.at[2], sum_r.at[2], (dev, d))

    def block(cycle, origin):
        return g.at[1, origin] if cycle else shares.at[origin]

    def tell(i, cycle):
        dev = sibling if i == 0 else lax.rem(d + 2 * i, domains)
        src = block(cycle, d)
        return remote(src, src, share_s.at[cycle, i], share_r.at[cycle, i], (b, dev))

    def origin_of(i, near):
        return sibling if i == 0 else lax.rem(near + (domains - 2 * i), domains)

    def told(i, cycle):
        origin = origin_of(i, d)
        src = block(cycle, origin)
        return remote(src, src, share_s.at[cycle, i], share_r.at[cycle, i], (b, origin))

    def hand_on(i, cycle):
        src = block(cycle, origin_of(i, d))
        return remote(src, src, pass_s.at[cycle, i], pass_r.at[cycle, i], (b, sibling))

    def handed(i, cycle):
        src = block(cycle, origin_of(i, sibling))
        return remote(src, src, pass_s.at[cycle, i], pass_r.at[cycle, i], (b, sibling))

    def make_share():
        first(va, vb, 0, *window(1))
        share[0] = packed(vb, va, OWN, OWN + 2)
        share[1] = packed(vb, va, OWN - 2, OWN + 4)

    def gather_share(at_centre):
        @pl.when(has_outer)
        def _():
            sum_up().wait_recv()
            share[...] = share[...] + share_outer[...]

        (sum_mid() if at_centre else sum_up()).start()

    def spread_share(at_centre):
        if at_centre:
            sum_mid().wait_recv()
            shares[d] = share[...] + share_inner[...]
        else:
            sum_down(inner).wait_recv()

        @pl.when(has_outer)
        def _():
            sum_down(outer).start()

        for i in range(chips):
            tell(i, 0).start()

    order = list(range(EARLY)) + [None] + list(range(EARLY, CHUNKS))

    def gather_step(n, at_centre):
        if order[n] is None:
            gather_share(at_centre)
        else:
            gathered(order[n], at_centre)

    def spread_step(n, at_centre):
        if order[n] is None:
            spread_share(at_centre)
        else:
            spread(order[n], at_centre)

    def total_share(e, j):
        below = shares[jnp.maximum(e - 1, 0), 1] * jnp.where(e > 0, 1.0, 0.0)
        above = shares[jnp.minimum(e + 1, domains - 1), 1] * jnp.where(e < domains - 1, 1.0, 0.0)
        a = shares[e, 0] + jnp.where(even, pltpu.roll(below, NX - 1, 1), pltpu.roll(above, 1, 1))
        f1[1 + 2 * e, PAD:PAD + rows1, :] = jnp.where(even, a, pltpu.roll(a, 1, 1))
        f1[2 + 2 * e, PAD:PAD + rows1, :] = jnp.where(even, pltpu.roll(a, NX - 1, 1), a)

    def gathered_shares():
        told(0, 0).wait_recv()
        for i in range(1, chips):
            handed(i, 0).wait_recv()
        loop(0, domains, total_share, 2)

    def gathered_residuals():
        for i in range(1, chips):
            told(i, 1).wait_recv()
            hand_on(i, 1).start()
        unpack(1, d)
        for i in range(1, chips):
            unpack(1, origin_of(i, d))
        told(0, 1).wait_recv()
        unpack(1, sibling)
        for i in range(1, chips):
            handed(i, 1).wait_recv()
            unpack(1, origin_of(i, sibling))

    def unpack(cycle, origin):
        a = g[cycle, origin]
        f1[1 + 2 * origin, PAD:PAD + rows1, :] = jnp.where(even, a, pltpu.roll(a, 1, 1))
        f1[2 + 2 * origin, PAD:PAD + rows1, :] = jnp.where(even, pltpu.roll(a, NX - 1, 1), a)

    def widen(a, level):
        width = 1 << level
        lane = lax.broadcasted_iota(jnp.int32, a.shape, 1)
        low = (lane // width) % 2 == 0
        return 0.5 * (a + jnp.where(low, pltpu.roll(a, NX - width, 1), pltpu.roll(a, width, 1)))

    def add_rows(dst, p, value, n):
        for odd in range(2):
            at = (p, pl.ds(PAD + odd, n, stride=2), slice(None))
            dst[at] = dst[at] + value

    def coarse(arrive, near, between):
        arrive()
        first(f1, u1a, 1, 1, n1)

        def down1(q, j):
            f2[1 + q, PAD:PAD + NY // 4, :] = widen(pooled(u1a, f1, 1, 1 + 2 * q, spare[j]), 1)

        loop(0, n2, down1)
        between()
        first(f2, u2a, 2, 1, n2)
        rows3 = NY // 8

        def down2(q, j):
            f3[pl.ds(pl.multiple_of(q * rows3, 8), rows3), :] = widen(pooled(u2a, f2, 2, 1 + 2 * q, spare[j]), 2)

        loop(0, n3, down2)
        dot = functools.partial(
            jnp.dot, precision=lax.Precision.HIGHEST, preferred_element_type=jnp.float32
        )
        modes = dot(left[...], dot(f3[...], into[...])) * weight[...]
        f3[...] = dot(dot(left[...], modes), back[...])

        def back2(q, j):
            value = f3[pl.ds(pl.multiple_of(q * rows3, 8), rows3), :]
            add_rows(u2a, 1 + 2 * q, value, rows3)
            add_rows(u2a, 2 + 2 * q, value, rows3)

        loop(0, n3, back2)
        sweep(u2a, f2, u2b, 2, 1, n2)
        sweep(u2b, f2, u2a, 2, 1, n2)

        def back1(q, j):
            value = u2a[1 + q, PAD:PAD + NY // 4, :]
            add_rows(u1a, 1 + 2 * q, value, NY // 4)
            add_rows(u1a, 2 + 2 * q, value, NY // 4)

        loop(0, n2, back1)
        for extra, src, dst in ((1, u1a, u1b), (0, u1b, u1a)):
            count = min(n1, 2 + 2 * (near + extra))
            start = jnp.clip(2 * d - near - extra, 0, n1 - count)
            sweep(src, f1, dst, 1, start + 1, count)

    def correct(v, planes):
        for p in planes:
            j = (p - OWN) // 2
            z = 2 * d + j

            @pl.when(jnp.logical_and(z >= 0, z < n1))
            def _():
                add_rows(v, p, u1a[z + 1, PAD:PAD + rows1, :], rows1)

    @pl.when(jnp.logical_not(centre))
    def _():
        for n in range(EARLY):
            gather_step(n, False)

    for c in range(EARLY, CHUNKS):
        density(c)
    make_share()

    @pl.when(centre)
    def _():
        for n in range(len(order) + LAG):
            if n < len(order):
                gather_step(n, True)
            if n >= LAG:
                spread_step(n - LAG, True)

    @pl.when(jnp.logical_not(centre))
    def _():
        for n in range(EARLY, len(order)):
            gather_step(n, False)
        for n in range(len(order)):
            spread_step(n, False)

    for i in range(1, chips):
        told(i, 0).wait_recv()
        hand_on(i, 0).start()

    def near_arrived():
        for c in range(CHUNKS):
            @pl.when(d < domains - 1)
            def _():
                near_down(c).wait_recv()

            @pl.when(d > 0)
            def _():
                near_up(c).wait_recv()

        for i in range(2):
            @pl.when(onward[i][4])
            def _():
                for h in range(HALVES):
                    onward_copy(i, h).start()

        for table in tables[1:]:
            table.wait()

    coarse(gathered_shares, 3, near_arrived)
    first(fx, vb, 0, *window(1))
    correct(vb, range(OWN - 1, OWN + 5))
    sweep(vb, fx, va, 0, *window(0))

    for i in range(4):
        @pl.when(far[i][4])
        def _():
            for h in range(HALVES):
                far_copy(i, h).wait_recv()

    first(fx, vb, 0, OWN - 5, 4)
    first(fx, vb, 0, OWN + PLANES + 1, 4)
    correct(vb, [*range(OWN - 5, OWN - 1), *range(OWN + 5, OWN + 9)])
    sweep(vb, fx, va, 0, OWN - 4, 4)
    sweep(vb, fx, va, 0, OWN + 4, 4)
    sweep(va, fx, vb, 0, *window(3))

    sweep(vb, fx, va, 0, *window(2))
    sweep(va, fx, vc, 0, *window(1))
    restrict_and_send(vc, 1)

    def v_up():
        return remote(
            vc.at[pl.ds(OWN + 2, 2), pl.ds(PAD, NY), :], hv.at[0], hv_s.at[0], hv_r.at[0], (b, d + 1)
        )

    def v_down():
        return remote(
            vc.at[pl.ds(OWN, 2), pl.ds(PAD, NY), :], hv.at[1], hv_s.at[1], hv_r.at[1], (b, d - 1)
        )

    @pl.when(d < domains - 1)
    def _():
        v_up().start()

    @pl.when(d > 0)
    def _():
        v_down().start()

    coarse(gathered_residuals, 1, lambda: None)

    @pl.when(d < domains - 1)
    def _():
        v_up().wait_send()
        v_down().wait_recv()
        vc[OWN + 4:OWN + 6, PAD:PAD + NY, :] = hv[1]

    @pl.when(d > 0)
    def _():
        v_down().wait_send()
        v_up().wait_recv()
        vc[OWN - 2:OWN, PAD:PAD + NY, :] = hv[0]

    for c in range(CHUNKS):
        @pl.when(centre)
        def _():
            mid(c).wait_send()

        @pl.when(jnp.logical_not(centre))
        def _():
            up(c).wait_send()

    correct(vc, range(OWN - 2, OWN + 6))
    sweep(vc, fx, va, 0, *window(1))
    for k, (r0, rn) in enumerate(blocks(0)):
        for p in range(PLANES):
            c, total = beside(va, OWN + p, r0, rn, 1)
            f = fx[OWN + p, PAD + r0:PAD + r0 + rn, :]
            mixed[pl.ds(r0 * PLANES + p, rn, stride=PLANES), :] = KEEP * c + GAIN[0] * (f + total)
        result(k).start()
    for k in range(len(blocks(0))):
        result(k).wait()

    for c in range(CHUNKS):
        @pl.when(has_outer)
        def _():
            down(c, outer).wait_send()

        @pl.when(d < domains - 1)
        def _():
            near_up(c).wait_send()

        @pl.when(d > 0)
        def _():
            near_down(c).wait_send()

    for i in range(4):
        @pl.when(far[i][3])
        def _():
            for h in range(HALVES):
                far_copy(i, h).wait_send()

    for i in range(2):
        @pl.when(onward[i][4])
        def _():
            for h in range(HALVES):
                onward_copy(i, h).wait_send()

    for cycle in range(2):
        for i in range(chips):
            tell(i, cycle).wait_send()
        for i in range(1, chips):
            hand_on(i, cycle).wait_send()

    @pl.when(centre)
    def _():
        sum_mid().wait_send()

    @pl.when(jnp.logical_not(centre))
    def _():
        sum_up().wait_send()

    @pl.when(has_outer)
    def _():
        sum_down(outer).wait_send()


def potential_of(orbitals, occupations, bands, domains):
    n1, n2, n3 = 2 * domains, domains, domains // 2
    tables = coarse_basis(n3)
    f32 = jnp.float32
    count = orbitals.shape[0]
    pair = pltpu.VMEM((2, NY // 2, NX), f32)
    slab = pltpu.VMEM((PLANES, NY, NX), f32)
    fine = pltpu.VMEM((WINDOW, NY + 2 * PAD, NX), f32)
    level1 = pltpu.VMEM((n1 + 2, NY // 2 + 2 * PAD, NX), f32)
    level2 = pltpu.VMEM((n2 + 2, NY // 4 + 2 * PAD, NX), f32)
    chunk_sems = pltpu.SemaphoreType.DMA((CHUNKS,))
    near_sems = pltpu.SemaphoreType.DMA((2, CHUNKS))
    sum_sems = pltpu.SemaphoreType.DMA((3,))
    chip_sems = pltpu.SemaphoreType.DMA((2, domains // 2))
    return pl.pallas_call(
        functools.partial(kernel, bands, domains, 0.5 * charge_scale / (count * bands)),
        out_shape=jax.ShapeDtypeStruct((ROOM, NX), f32),
        in_specs=[pl.BlockSpec(memory_space=pl.ANY)] * 6,
        out_specs=pl.BlockSpec(memory_space=pl.ANY),
        scratch_shapes=[
            pltpu.SMEM(occupations.shape, jnp.int32),
            *[pltpu.VMEM(table.shape, f32) for table in tables],
            pltpu.VMEM(orbitals.shape, orbitals.dtype),
            pltpu.VMEM((NY * PLANES, NX), f32),
            pltpu.SemaphoreType.DMA((8,)), pltpu.SemaphoreType.DMA((5,)), chunk_sems,
            slab, slab, slab, fine, fine, fine, fine,
            pltpu.VMEM((2, 2, NY, NX), f32),
            *[pltpu.VMEM((NY, NX), f32)] * 4,
            pltpu.VMEM((2, domains, NY // 2, NX), f32),
            pair, pair, pair, pltpu.VMEM((domains, 2, NY // 2, NX), f32),
            level1, level1, level1, level2, level2, level2,
            pltpu.VMEM((n3 * (NY // 8), NX), f32),
            chunk_sems, chunk_sems, chunk_sems, chunk_sems, chunk_sems, chunk_sems,
            near_sems, near_sems,
            pltpu.SemaphoreType.DMA((6, HALVES)), pltpu.SemaphoreType.DMA((4, HALVES)),
            pltpu.SemaphoreType.DMA((2,)), pltpu.SemaphoreType.DMA((2,)),
            sum_sems, sum_sems, chip_sems, chip_sems, chip_sems, chip_sems,
        ],
        compiler_params=pltpu.CompilerParams(
            collective_id=0, has_side_effects=True, vmem_limit_bytes=62_500_000
        ),
    )(occupations, orbitals, *[jnp.asarray(table) for table in tables])


def apply(mixed_in, orbitals, potential, applied, mixed, held, in_s, keep_s, held_s):
    rows = STEP * PLANES

    def part(c):
        return (slice(None), pl.ds(c * rows, rows), slice(None))

    def fetch(c):
        at = pl.ds(c * rows, rows)
        return pltpu.make_async_copy(mixed_in.at[at], mixed.at[at], in_s.at[c])

    def keep(c):
        at = pl.ds(c * rows, rows)
        return pltpu.make_async_copy(mixed.at[at], potential.at[at], keep_s.at[c])

    def store(c):
        return pltpu.make_async_copy(held.at[part(c)], applied.at[part(c)], held_s.at[c])

    for c in range(CHUNKS):
        fetch(c).start()
    for c in range(CHUNKS):
        fetch(c).wait()
        keep(c).start()
        value = mixed[c * rows:(c + 1) * rows, :]
        for i in range(orbitals.shape[0]):
            psi = orbitals[i, c * rows:(c + 1) * rows, :].astype(jnp.float32)
            held[i, c * rows:(c + 1) * rows, :] = (value * psi).astype(held.dtype)
        store(c).start()
    for c in range(CHUNKS):
        keep(c).wait()
        store(c).wait()


def cells_of(orbitals):
    count = orbitals.shape[0]
    cells = orbitals.reshape(count, PLANES, NY, NX).transpose(0, 2, 1, 3)
    return cells.reshape(count, NY * PLANES, NX)


def applied_of(mixed, cells):
    sems = pltpu.SemaphoreType.DMA((CHUNKS,))
    anywhere = pl.BlockSpec(memory_space=pl.ANY)
    count = cells.shape[0]
    potential, applied = pl.pallas_call(
        apply,
        out_shape=(
            jax.ShapeDtypeStruct((NY * PLANES, NX), jnp.float32),
            jax.ShapeDtypeStruct(cells.shape, cells.dtype),
        ),
        in_specs=[anywhere, pl.BlockSpec(memory_space=pltpu.VMEM)],
        out_specs=(anywhere, anywhere),
        scratch_shapes=[
            pltpu.VMEM((NY * PLANES, NX), jnp.float32),
            pltpu.VMEM(cells.shape, cells.dtype),
            sems, sems, sems,
        ],
        compiler_params=pltpu.CompilerParams(vmem_limit_bytes=54_200_000),
    )(mixed, cells)
    applied = applied.reshape(count, NY, PLANES, NX).transpose(0, 2, 1, 3)
    potential = potential.reshape(NY, PLANES, NX).transpose(1, 0, 2)
    return potential.reshape(PLANES, NY * NX), applied.reshape(count, PLANES, NY * NX)


def body(bands, domains, orbitals, occupations):
    cells = cells_of(orbitals)
    return applied_of(potential_of(cells, occupations, bands, domains), cells)


def solution(mesh):
    return jax.shard_map(
        functools.partial(body, mesh.shape["band"], mesh.shape["dom"]),
        mesh=mesh,
        in_specs=(P("band", "dom", None), P("band")),
        out_specs=(P("dom", None), P("band", "dom", None)),
        check_vma=False,
    )
```

```python
import functools

import jax
import jax.numpy as jnp
import numpy as np
from jax import lax
from jax.experimental import pallas as pl
from jax.experimental.pallas import tpu as pltpu
from jax.sharding import PartitionSpec as P

NX = 128
NY = 192
COARSE = 48

screening = 0.02
relaxation = 0.8
charge_scale = 0.07

PLANES = 4
HALO = 6
OWN = HALO
WINDOW = PLANES + 2 * HALO
PAD = 8
CHUNKS = 8
LAG = 3
EARLY = 2
ROOM = 8192
HALVES = 2
MOST = (4, 4, 8)
STEP = NY // CHUNKS
HALF = NY // HALVES
CENTRE = [6.0 + screening * 4.0**level for level in range(4)]
GAIN = [relaxation / centre for centre in CENTRE]
KEEP = 1.0 - relaxation


def sines(n):
    k = np.arange(1, n + 1)
    basis = np.sqrt(2.0 / (n + 1)) * np.sin(np.pi * np.outer(k, k) / (n + 1))
    return basis, 2.0 * np.cos(np.pi * k / (n + 1))


def coarse_basis(depth):
    rows, cols, copies = NY // 8, NX // 8, 8
    sz, ez = sines(depth)
    sy, ey = sines(rows)
    sx, ex = sines(cols)
    left = np.kron(sz, sy)
    into = np.zeros((NX, NX))
    into[::copies, :cols] = sx
    back = np.zeros((NX, NX))
    back[:cols] = np.repeat(sx, copies, axis=1)
    near = (ez[:, None] + ey[None, :]).reshape(-1, 1) + ex[None, :]
    rate = KEEP + GAIN[3] * near
    total = GAIN[3] * sum(rate**n for n in range(COARSE))
    weight = np.zeros((depth * rows, NX))
    weight[:, :cols] = total
    return [np.asarray(part, np.float32) for part in (left, into, back, weight)]


def kernel(
    bands, domains, scale,
    occupations, orbitals, left_in, into_in, back_in, weight_in,
    out,
    occ, left, into, back, weight, held, mixed, out_s, table_s, held_s,
    acc, from_outer, from_inner, fx, va, vb, vc, hv, t0, t1, t2, t3, g,
    share, share_outer, share_inner, shares,
    f1, u1a, u1b, f2, u2a, u2b, f3,
    up_s, up_r, mid_s, mid_r, down_s, down_r, near_s, near_r, far_s, far_r, hv_s, hv_r,
    sum_s, sum_r, share_s, share_r, pass_s, pass_r,
):
    b = lax.axis_index("band")
    d = lax.axis_index("dom")
    half = bands // 2
    lower = b < half
    inner = jnp.where(lower, b + 1, b - 1)
    outer = jnp.where(lower, b - 1, b + 1)
    has_outer = jnp.logical_and(b > 0, b < bands - 1)
    centre = jnp.logical_or(b == half - 1, b == half)
    n1, n2, n3 = 2 * domains, domains, domains // 2

    def remote(src, dst, ss, rs, dev):
        return pltpu.make_async_remote_copy(
            src_ref=src, dst_ref=dst, send_sem=ss, recv_sem=rs,
            device_id=dev, device_id_type=pl.DeviceIdType.MESH,
        )

    lines = STEP * PLANES

    def fetch(c):
        at = (slice(None), pl.ds(c * lines, lines), slice(None))
        return pltpu.make_async_copy(orbitals.at[at], held.at[at], held_s.at[c])

    def result(p):
        r0, rn = blocks(0)[p]
        rows = pl.ds(r0 * PLANES, rn * PLANES)
        return pltpu.make_async_copy(mixed.at[rows], out.at[rows], out_s.at[p])

    tables = [
        pltpu.make_async_copy(src, dst, table_s.at[i])
        for i, (src, dst) in enumerate(
            ((occupations, occ), (left_in, left), (into_in, into), (back_in, back), (weight_in, weight))
        )
    ]
    tables[0].start()
    for c in range(CHUNKS):
        fetch(c).start()
    for table in tables[1:]:
        table.start()
    barrier = pltpu.get_barrier_semaphore()

    def greet(dev):
        pl.semaphore_signal(barrier, inc=1, device_id=dev, device_id_type=pl.DeviceIdType.MESH)

    for i in range(1, domains):
        greet((b, lax.rem(d + i, domains)))
    greet((inner, d))

    @pl.when(has_outer)
    def _():
        greet((outer, d))

    for ref in (fx, va, vb, vc, f1, u1a, u1b, f2, u2a, u2b):
        edge = jnp.zeros((ref.shape[0], PAD, NX), jnp.float32)
        ref[:, 0:PAD, :] = edge
        ref[:, ref.shape[1] - PAD:ref.shape[1], :] = edge

    def clear(ref, p):
        ref[p] = jnp.zeros(ref.shape[1:], jnp.float32)

    for ref in (f1, u1a, u1b, f2, u2a, u2b):
        clear(ref, 0)
        clear(ref, ref.shape[0] - 1)
    clear(vc, OWN - 2)
    clear(vc, OWN + 5)
    for p in (OWN - 2, OWN - 1, OWN + 4, OWN + 5):
        clear(va, p)
    for p in (OWN - 3, OWN - 2, OWN + 5, OWN + 6):
        clear(vb, p)
    for k in range(HALO):
        reach = -(-(HALO - k) // PLANES)

        @pl.when(d < reach)
        def _():
            clear(fx, k)

        @pl.when(d >= domains - reach)
        def _():
            clear(fx, WINDOW - 1 - k)

    def density(c):
        fetch(c).wait()
        first_row = c * lines
        total = None
        for i in range(orbitals.shape[0]):
            value = held[i, first_row:first_row + lines, :].astype(jnp.float32)
            term = (occ[i].astype(jnp.float32) * scale) * (value * value)
            total = term if total is None else total + term
        mixed[first_row:first_row + lines, :] = total
        for p in range(PLANES):
            plane = mixed[pl.ds(first_row + p, STEP, stride=PLANES), :]
            acc[p, c * STEP:(c + 1) * STEP, :] = plane
            va[OWN + p, PAD + c * STEP:PAD + (c + 1) * STEP, :] = plane

    tables[0].wait()
    for c in range(EARLY):
        density(c)
    pl.semaphore_wait(barrier, domains + jnp.where(has_outer, 1, 0))

    def part(ref, c):
        return ref.at[:, pl.ds(c * STEP, STEP), :]

    def slab(c):
        return fx.at[pl.ds(OWN, PLANES), pl.ds(PAD + c * STEP, STEP), :]

    def up(c):
        return remote(part(acc, c), part(from_outer, c), up_s.at[c], up_r.at[c], (inner, d))

    def mid(c):
        return remote(part(acc, c), part(from_inner, c), mid_s.at[c], mid_r.at[c], (inner, d))

    def down(c, dev):
        return remote(slab(c), slab(c), down_s.at[c], down_r.at[c], (dev, d))

    def near_up(c):
        rows = pl.ds(PAD + c * STEP, STEP)
        return remote(
            fx.at[pl.ds(OWN + 2, 2), rows, :], fx.at[pl.ds(OWN - 2, 2), rows, :],
            near_s.at[0, c], near_r.at[0, c], (b, d + 1),
        )

    def near_down(c):
        rows = pl.ds(PAD + c * STEP, STEP)
        return remote(
            fx.at[pl.ds(OWN, 2), rows, :], fx.at[pl.ds(OWN + 4, 2), rows, :],
            near_s.at[1, c], near_r.at[1, c], (b, d - 1),
        )

    even_d = lax.rem(d, 2) == 0
    odd_d = lax.rem(d, 2) == 1
    far = [
        (OWN, OWN - 4, 1, d < domains - 1, d > 0),
        (OWN + 2, OWN + 6, -1, d > 0, d < domains - 1),
        (OWN + 2, OWN - 6, 2, jnp.logical_and(even_d, d < domains - 2), d > 1),
        (OWN, OWN + 8, -2, jnp.logical_and(odd_d, d > 1), d < domains - 2),
    ]

    def far_copy(i, h):
        at, to, offset, _, _ = far[i]
        rows = pl.ds(PAD + h * HALF, HALF)
        return remote(
            fx.at[pl.ds(at, 2), rows, :], fx.at[pl.ds(to, 2), rows, :],
            far_s.at[i, h], far_r.at[i, h], (b, d + offset),
        )

    onward = [
        (OWN - 2, OWN - 6, 1, 2, jnp.logical_and(even_d, d > 1)),
        (OWN + 4, OWN + 8, -1, 3, jnp.logical_and(odd_d, d < domains - 2)),
    ]

    def onward_copy(i, h):
        at, to, offset, slot, _ = onward[i]
        rows = pl.ds(PAD + h * HALF, HALF)
        return remote(
            fx.at[pl.ds(at, 2), rows, :], fx.at[pl.ds(to, 2), rows, :],
            far_s.at[slot + 2, h], far_r.at[slot, h], (b, d + offset),
        )

    def gathered(c, at_centre):
        rows = slice(c * STEP, (c + 1) * STEP)

        @pl.when(has_outer)
        def _():
            up(c).wait_recv()
            acc[:, rows, :] = acc[:, rows, :] + from_outer[:, rows, :]

        (mid(c) if at_centre else up(c)).start()

    def spread(c, at_centre):
        rows = slice(c * STEP, (c + 1) * STEP)
        if at_centre:
            mid(c).wait_recv()
            fx[OWN:OWN + PLANES, PAD + c * STEP:PAD + (c + 1) * STEP, :] = (
                acc[:, rows, :] + from_inner[:, rows, :]
            )
        else:
            down(c, inner).wait_recv()

        @pl.when(has_outer)
        def _():
            down(c, outer).start()

        @pl.when(d < domains - 1)
        def _():
            near_up(c).start()

        @pl.when(d > 0)
        def _():
            near_down(c).start()

        if (c + 1) % (CHUNKS // HALVES) == 0:
            for i in range(4):
                @pl.when(far[i][3])
                def _():
                    far_copy(i, c // (CHUNKS // HALVES)).start()

    def beside(src, p, r0, rn, width):
        c = src[p, PAD + r0:PAD + r0 + rn, :]
        lane = lax.broadcasted_iota(jnp.int32, (rn, NX), 1)
        total = src[p, PAD + r0 - 1:PAD + r0 + rn - 1, :] + src[p, PAD + r0 + 1:PAD + r0 + rn + 1, :]
        total = total + (src[p - 1, PAD + r0:PAD + r0 + rn, :] + src[p + 1, PAD + r0:PAD + r0 + rn, :])
        total = total + jnp.where(lane < width, 0.0, pltpu.roll(c, width, 1))
        total = total + jnp.where(lane >= NX - width, 0.0, pltpu.roll(c, NX - width, 1))
        return c, total

    def rows_of(level):
        return NY >> level

    def blocks(level):
        rn = 48 if rows_of(level) % 48 == 0 else rows_of(level)
        return [(r0, rn) for r0 in range(0, rows_of(level), rn)]

    def loop(lo, count, fn, most=4):
        group = max(n for n in range(1, most + 1) if count % n == 0)

        def step(i, carry):
            for j in range(group):
                fn(lo + i * group + j, j)
            return carry

        lax.fori_loop(0, count // group, step, 0)

    def gain(level, p):
        if level:
            return GAIN[level]
        z = PLANES * d - OWN + p
        inside = jnp.logical_and(z >= 0, z < PLANES * domains)
        return jnp.where(inside, jnp.float32(GAIN[0]), jnp.float32(0.0))

    def first(src, dst, level, lo, count):
        def plane(p, j):
            k = gain(level, p)
            for r0, rn in blocks(level):
                c, total = beside(src, p, r0, rn, 1 << level)
                dst[p, PAD + r0:PAD + r0 + rn, :] = (GAIN[level] * (1.0 + KEEP)) * c + (k * GAIN[level]) * total

        loop(lo, count, plane, MOST[level])

    def sweep(src, source, dst, level, lo, count):
        def plane(p, j):
            k = gain(level, p)
            for r0, rn in blocks(level):
                c, total = beside(src, p, r0, rn, 1 << level)
                f = source[p, PAD + r0:PAD + r0 + rn, :]
                dst[p, PAD + r0:PAD + r0 + rn, :] = KEEP * c + k * (f + total)

        loop(lo, count, plane, MOST[level])

    def residual(v, source, level, p, r0, rn):
        c, total = beside(v, p, r0, rn, 1 << level)
        return source[p, PAD + r0:PAD + r0 + rn, :] + total - CENTRE[level] * c

    spare = (t0, t1, t2, t3)

    def pooled(v, source, level, p, t):
        for r0, rn in blocks(level):
            t[r0:r0 + rn, :] = residual(v, source, level, p, r0, rn) + residual(v, source, level, p + 1, r0, rn)
        n = rows_of(level) // 2
        return t[pl.ds(0, n, stride=2), :] + t[pl.ds(1, n, stride=2), :]

    def window(h):
        return OWN - h, PLANES + 2 * h

    rows1 = NY // 2
    even = lax.broadcasted_iota(jnp.int32, (rows1, NX), 1) % 2 == 0

    def packed(v, source, at, to):
        a = pooled(v, source, 0, at, t0)
        a = a + pltpu.roll(a, NX - 1, 1)
        e = pooled(v, source, 0, to, t1)
        e = e + pltpu.roll(e, 1, 1)
        return 0.5 * jnp.where(even, a, e)

    def restrict_and_send(v, cycle):
        for slot in (1, 2):
            low = (slot - 1) * NY // 2
            pairs = []
            for at, t in ((OWN, t0), (OWN + 2, t1)):
                for r0 in range(low, low + NY // 2, 48):
                    t[r0:r0 + 48, :] = residual(v, fx, 0, at, r0, 48) + residual(v, fx, 0, at + 1, r0, 48)
                n = rows1 // 2
                pairs.append(t[pl.ds(low, n, stride=2), :] + t[pl.ds(low + 1, n, stride=2), :])
            a = pairs[0] + pltpu.roll(pairs[0], NX - 1, 1)
            e = pairs[1] + pltpu.roll(pairs[1], 1, 1)
            g[cycle, d, low // 2:low // 2 + n, :] = 0.5 * jnp.where(even[:n], a, e)
            for i in range(1, chips):
                tell(i, slot).start()
            tell(0, slot).start()

    sibling = d + 1 - 2 * lax.rem(d, 2)
    chips = domains // 2

    def sum_up():
        return remote(share, share_outer, sum_s.at[0], sum_r.at[0], (inner, d))

    def sum_mid():
        return remote(share, share_inner, sum_s.at[1], sum_r.at[1], (inner, d))

    def sum_down(dev):
        return remote(shares.at[d], shares.at[d], sum_s.at[2], sum_r.at[2], (dev, d))

    def block(cycle, origin):
        if cycle == 0:
            return shares.at[origin]
        return g.at[1, origin, pl.ds((cycle - 1) * (rows1 // 2), rows1 // 2), :]

    def tell(i, cycle):
        dev = sibling if i == 0 else lax.rem(d + 2 * i, domains)
        src = block(cycle, d)
        return remote(src, src, share_s.at[cycle, i], share_r.at[cycle, i], (b, dev))

    def origin_of(i, near):
        return sibling if i == 0 else lax.rem(near + (domains - 2 * i), domains)

    def told(i, cycle):
        origin = origin_of(i, d)
        src = block(cycle, origin)
        return remote(src, src, share_s.at[cycle, i], share_r.at[cycle, i], (b, origin))

    def hand_on(i, cycle):
        src = block(cycle, origin_of(i, d))
        return remote(src, src, pass_s.at[cycle, i], pass_r.at[cycle, i], (b, sibling))

    def handed(i, cycle):
        src = block(cycle, origin_of(i, sibling))
        return remote(src, src, pass_s.at[cycle, i], pass_r.at[cycle, i], (b, sibling))

    def make_share():
        first(va, vb, 0, *window(1))
        share[0] = packed(vb, va, OWN, OWN + 2)
        share[1] = packed(vb, va, OWN - 2, OWN + 4)

    def gather_share(at_centre):
        @pl.when(has_outer)
        def _():
            sum_up().wait_recv()
            share[...] = share[...] + share_outer[...]

        (sum_mid() if at_centre else sum_up()).start()

    def spread_share(at_centre):
        if at_centre:
            sum_mid().wait_recv()
            shares[d] = share[...] + share_inner[...]
        else:
            sum_down(inner).wait_recv()

        @pl.when(has_outer)
        def _():
            sum_down(outer).start()

        for i in range(chips):
            tell(i, 0).start()

    order = list(range(EARLY)) + [None] + list(range(EARLY, CHUNKS))

    def gather_step(n, at_centre):
        if order[n] is None:
            gather_share(at_centre)
        else:
            gathered(order[n], at_centre)

    def spread_step(n, at_centre):
        if order[n] is None:
            spread_share(at_centre)
        else:
            spread(order[n], at_centre)

    def total_share(e, j):
        below = shares[jnp.maximum(e - 1, 0), 1] * jnp.where(e > 0, 1.0, 0.0)
        above = shares[jnp.minimum(e + 1, domains - 1), 1] * jnp.where(e < domains - 1, 1.0, 0.0)
        a = shares[e, 0] + jnp.where(even, pltpu.roll(below, NX - 1, 1), pltpu.roll(above, 1, 1))
        f1[1 + 2 * e, PAD:PAD + rows1, :] = jnp.where(even, a, pltpu.roll(a, 1, 1))
        f1[2 + 2 * e, PAD:PAD + rows1, :] = jnp.where(even, pltpu.roll(a, NX - 1, 1), a)

    def gathered_shares():
        told(0, 0).wait_recv()
        for i in range(1, chips):
            handed(i, 0).wait_recv()
        loop(0, domains, total_share, 2)

    def v_up():
        return remote(
            vc.at[pl.ds(OWN + 2, 2), pl.ds(PAD, NY), :], hv.at[0], hv_s.at[0], hv_r.at[0], (b, d + 1)
        )

    def v_down():
        return remote(
            vc.at[pl.ds(OWN, 2), pl.ds(PAD, NY), :], hv.at[1], hv_s.at[1], hv_r.at[1], (b, d - 1)
        )

    def gathered_residuals():
        for slot in (1, 2):
            for i in range(1, chips):
                told(i, slot).wait_recv()
                hand_on(i, slot).start()

        @pl.when(d < domains - 1)
        def _():
            v_up().start()

        @pl.when(d > 0)
        def _():
            v_down().start()

        unpack(1, d)
        for i in range(1, chips):
            unpack(1, origin_of(i, d))
        told(0, 1).wait_recv()
        told(0, 2).wait_recv()
        unpack(1, sibling)
        for i in range(1, chips):
            handed(i, 1).wait_recv()
            handed(i, 2).wait_recv()
            unpack(1, origin_of(i, sibling))

    def unpack(cycle, origin):
        a = g[cycle, origin]
        f1[1 + 2 * origin, PAD:PAD + rows1, :] = jnp.where(even, a, pltpu.roll(a, 1, 1))
        f1[2 + 2 * origin, PAD:PAD + rows1, :] = jnp.where(even, pltpu.roll(a, NX - 1, 1), a)

    def widen(a, level):
        width = 1 << level
        lane = lax.broadcasted_iota(jnp.int32, a.shape, 1)
        low = (lane // width) % 2 == 0
        return 0.5 * (a + jnp.where(low, pltpu.roll(a, NX - width, 1), pltpu.roll(a, width, 1)))

    def add_rows(dst, p, value, n):
        for odd in range(2):
            at = (p, pl.ds(PAD + odd, n, stride=2), slice(None))
            dst[at] = dst[at] + value

    def coarse(arrive, near, between):
        arrive()
        first(f1, u1a, 1, 1, n1)

        def down1(q, j):
            f2[1 + q, PAD:PAD + NY // 4, :] = widen(pooled(u1a, f1, 1, 1 + 2 * q, spare[j]), 1)

        loop(0, n2, down1)
        between()
        first(f2, u2a, 2, 1, n2)
        rows3 = NY // 8

        def down2(q, j):
            f3[pl.ds(pl.multiple_of(q * rows3, 8), rows3), :] = widen(pooled(u2a, f2, 2, 1 + 2 * q, spare[j]), 2)

        loop(0, n3, down2)
        dot = functools.partial(
            jnp.dot, precision=lax.Precision.HIGHEST, preferred_element_type=jnp.float32
        )
        modes = dot(left[...], dot(f3[...], into[...])) * weight[...]
        f3[...] = dot(dot(left[...], modes), back[...])

        def back2(q, j):
            value = f3[pl.ds(pl.multiple_of(q * rows3, 8), rows3), :]
            add_rows(u2a, 1 + 2 * q, value, rows3)
            add_rows(u2a, 2 + 2 * q, value, rows3)

        loop(0, n3, back2)
        sweep(u2a, f2, u2b, 2, 1, n2)
        sweep(u2b, f2, u2a, 2, 1, n2)

        def back1(q, j):
            value = u2a[1 + q, PAD:PAD + NY // 4, :]
            add_rows(u1a, 1 + 2 * q, value, NY // 4)
            add_rows(u1a, 2 + 2 * q, value, NY // 4)

        loop(0, n2, back1)
        for extra, src, dst in ((1, u1a, u1b), (0, u1b, u1a)):
            count = min(n1, 2 + 2 * (near + extra))
            start = jnp.clip(2 * d - near - extra, 0, n1 - count)
            sweep(src, f1, dst, 1, start + 1, count)

    def correct(v, planes):
        for p in planes:
            j = (p - OWN) // 2
            z = 2 * d + j

            @pl.when(jnp.logical_and(z >= 0, z < n1))
            def _():
                add_rows(v, p, u1a[z + 1, PAD:PAD + rows1, :], rows1)

    @pl.when(jnp.logical_not(centre))
    def _():
        for n in range(EARLY):
            gather_step(n, False)

    for c in range(EARLY, CHUNKS):
        density(c)
    make_share()

    @pl.when(centre)
    def _():
        for n in range(len(order) + LAG):
            if n < len(order):
                gather_step(n, True)
            if n >= LAG:
                spread_step(n - LAG, True)

    @pl.when(jnp.logical_not(centre))
    def _():
        for n in range(EARLY, len(order)):
            gather_step(n, False)
        for n in range(len(order)):
            spread_step(n, False)

    for i in range(1, chips):
        told(i, 0).wait_recv()
        hand_on(i, 0).start()

    def near_arrived():
        for c in range(CHUNKS):
            @pl.when(d < domains - 1)
            def _():
                near_down(c).wait_recv()

            @pl.when(d > 0)
            def _():
                near_up(c).wait_recv()

        for i in range(2):
            @pl.when(onward[i][4])
            def _():
                for h in range(HALVES):
                    onward_copy(i, h).start()

        for table in tables[1:]:
            table.wait()

    coarse(gathered_shares, 3, near_arrived)
    first(fx, vb, 0, *window(1))
    correct(vb, range(OWN - 1, OWN + 5))
    sweep(vb, fx, va, 0, *window(0))

    for i in range(4):
        @pl.when(far[i][4])
        def _():
            for h in range(HALVES):
                far_copy(i, h).wait_recv()

    first(fx, vb, 0, OWN - 5, 4)
    first(fx, vb, 0, OWN + PLANES + 1, 4)
    correct(vb, [*range(OWN - 5, OWN - 1), *range(OWN + 5, OWN + 9)])
    sweep(vb, fx, va, 0, OWN - 4, 4)
    sweep(vb, fx, va, 0, OWN + 4, 4)
    sweep(va, fx, vb, 0, *window(3))

    sweep(vb, fx, va, 0, *window(2))
    sweep(va, fx, vc, 0, *window(1))
    restrict_and_send(vc, 1)

    coarse(gathered_residuals, 1, lambda: None)

    @pl.when(d < domains - 1)
    def _():
        v_up().wait_send()
        v_down().wait_recv()
        vc[OWN + 4:OWN + 6, PAD:PAD + NY, :] = hv[1]

    @pl.when(d > 0)
    def _():
        v_down().wait_send()
        v_up().wait_recv()
        vc[OWN - 2:OWN, PAD:PAD + NY, :] = hv[0]

    for c in range(CHUNKS):
        @pl.when(centre)
        def _():
            mid(c).wait_send()

        @pl.when(jnp.logical_not(centre))
        def _():
            up(c).wait_send()

    correct(vc, range(OWN - 2, OWN + 6))
    sweep(vc, fx, va, 0, *window(1))
    for k, (r0, rn) in enumerate(blocks(0)):
        for p in range(PLANES):
            c, total = beside(va, OWN + p, r0, rn, 1)
            f = fx[OWN + p, PAD + r0:PAD + r0 + rn, :]
            mixed[pl.ds(r0 * PLANES + p, rn, stride=PLANES), :] = KEEP * c + GAIN[0] * (f + total)
        result(k).start()
    for k in range(len(blocks(0))):
        result(k).wait()

    for c in range(CHUNKS):
        @pl.when(has_outer)
        def _():
            down(c, outer).wait_send()

        @pl.when(d < domains - 1)
        def _():
            near_up(c).wait_send()

        @pl.when(d > 0)
        def _():
            near_down(c).wait_send()

    for i in range(4):
        @pl.when(far[i][3])
        def _():
            for h in range(HALVES):
                far_copy(i, h).wait_send()

    for i in range(2):
        @pl.when(onward[i][4])
        def _():
            for h in range(HALVES):
                onward_copy(i, h).wait_send()

    for cycle in range(3):
        for i in range(chips):
            tell(i, cycle).wait_send()
        for i in range(1, chips):
            hand_on(i, cycle).wait_send()

    @pl.when(centre)
    def _():
        sum_mid().wait_send()

    @pl.when(jnp.logical_not(centre))
    def _():
        sum_up().wait_send()

    @pl.when(has_outer)
    def _():
        sum_down(outer).wait_send()


def potential_of(orbitals, occupations, bands, domains):
    n1, n2, n3 = 2 * domains, domains, domains // 2
    tables = coarse_basis(n3)
    f32 = jnp.float32
    count = orbitals.shape[0]
    pair = pltpu.VMEM((2, NY // 2, NX), f32)
    slab = pltpu.VMEM((PLANES, NY, NX), f32)
    fine = pltpu.VMEM((WINDOW, NY + 2 * PAD, NX), f32)
    level1 = pltpu.VMEM((n1 + 2, NY // 2 + 2 * PAD, NX), f32)
    level2 = pltpu.VMEM((n2 + 2, NY // 4 + 2 * PAD, NX), f32)
    chunk_sems = pltpu.SemaphoreType.DMA((CHUNKS,))
    near_sems = pltpu.SemaphoreType.DMA((2, CHUNKS))
    sum_sems = pltpu.SemaphoreType.DMA((3,))
    chip_sems = pltpu.SemaphoreType.DMA((3, domains // 2))
    return pl.pallas_call(
        functools.partial(kernel, bands, domains, 0.5 * charge_scale / (count * bands)),
        out_shape=jax.ShapeDtypeStruct((ROOM, NX), f32),
        in_specs=[pl.BlockSpec(memory_space=pl.ANY)] * 6,
        out_specs=pl.BlockSpec(memory_space=pl.ANY),
        scratch_shapes=[
            pltpu.SMEM(occupations.shape, jnp.int32),
            *[pltpu.VMEM(table.shape, f32) for table in tables],
            pltpu.VMEM(orbitals.shape, orbitals.dtype),
            pltpu.VMEM((NY * PLANES, NX), f32),
            pltpu.SemaphoreType.DMA((8,)), pltpu.SemaphoreType.DMA((5,)), chunk_sems,
            slab, slab, slab, fine, fine, fine, fine,
            pltpu.VMEM((2, 2, NY, NX), f32),
            *[pltpu.VMEM((NY, NX), f32)] * 4,
            pltpu.VMEM((2, domains, NY // 2, NX), f32),
            pair, pair, pair, pltpu.VMEM((domains, 2, NY // 2, NX), f32),
            level1, level1, level1, level2, level2, level2,
            pltpu.VMEM((n3 * (NY // 8), NX), f32),
            chunk_sems, chunk_sems, chunk_sems, chunk_sems, chunk_sems, chunk_sems,
            near_sems, near_sems,
            pltpu.SemaphoreType.DMA((6, HALVES)), pltpu.SemaphoreType.DMA((4, HALVES)),
            pltpu.SemaphoreType.DMA((2,)), pltpu.SemaphoreType.DMA((2,)),
            sum_sems, sum_sems, chip_sems, chip_sems, chip_sems, chip_sems,
        ],
        compiler_params=pltpu.CompilerParams(
            collective_id=0, has_side_effects=True, vmem_limit_bytes=62_500_000
        ),
    )(occupations, orbitals, *[jnp.asarray(table) for table in tables])


def apply(mixed_in, orbitals, potential, applied, mixed, held, in_s, keep_s, held_s):
    rows = STEP * PLANES

    def part(c):
        return (slice(None), pl.ds(c * rows, rows), slice(None))

    def fetch(c):
        at = pl.ds(c * rows, rows)
        return pltpu.make_async_copy(mixed_in.at[at], mixed.at[at], in_s.at[c])

    def keep(c):
        at = pl.ds(c * rows, rows)
        return pltpu.make_async_copy(mixed.at[at], potential.at[at], keep_s.at[c])

    def store(c):
        return pltpu.make_async_copy(held.at[part(c)], applied.at[part(c)], held_s.at[c])

    for c in range(CHUNKS):
        fetch(c).start()
    for c in range(CHUNKS):
        fetch(c).wait()
        keep(c).start()
        value = mixed[c * rows:(c + 1) * rows, :]
        for i in range(orbitals.shape[0]):
            psi = orbitals[i, c * rows:(c + 1) * rows, :].astype(jnp.float32)
            held[i, c * rows:(c + 1) * rows, :] = (value * psi).astype(held.dtype)
        store(c).start()
    for c in range(CHUNKS):
        keep(c).wait()
        store(c).wait()


def cells_of(orbitals):
    count = orbitals.shape[0]
    cells = orbitals.reshape(count, PLANES, NY, NX).transpose(0, 2, 1, 3)
    return cells.reshape(count, NY * PLANES, NX)


def applied_of(mixed, cells):
    sems = pltpu.SemaphoreType.DMA((CHUNKS,))
    anywhere = pl.BlockSpec(memory_space=pl.ANY)
    count = cells.shape[0]
    potential, applied = pl.pallas_call(
        apply,
        out_shape=(
            jax.ShapeDtypeStruct((NY * PLANES, NX), jnp.float32),
            jax.ShapeDtypeStruct(cells.shape, cells.dtype),
        ),
        in_specs=[anywhere, pl.BlockSpec(memory_space=pltpu.VMEM)],
        out_specs=(anywhere, anywhere),
        scratch_shapes=[
            pltpu.VMEM((NY * PLANES, NX), jnp.float32),
            pltpu.VMEM(cells.shape, cells.dtype),
            sems, sems, sems,
        ],
        compiler_params=pltpu.CompilerParams(vmem_limit_bytes=54_200_000),
    )(mixed, cells)
    applied = applied.reshape(count, NY, PLANES, NX).transpose(0, 2, 1, 3)
    potential = potential.reshape(NY, PLANES, NX).transpose(1, 0, 2)
    return potential.reshape(PLANES, NY * NX), applied.reshape(count, PLANES, NY * NX)


def body(bands, domains, orbitals, occupations):
    cells = cells_of(orbitals)
    return applied_of(potential_of(cells, occupations, bands, domains), cells)


def solution(mesh):
    return jax.shard_map(
        functools.partial(body, mesh.shape["band"], mesh.shape["dom"]),
        mesh=mesh,
        in_specs=(P("band", "dom", None), P("band")),
        out_specs=(P("dom", None), P("band", "dom", None)),
        check_vma=False,
    )
```

```python
import functools

import jax
import jax.numpy as jnp
import numpy as np
from jax import lax
from jax.experimental import pallas as pl
from jax.experimental.pallas import tpu as pltpu
from jax.sharding import PartitionSpec as P

NX = 128
NY = 192
COARSE = 48

screening = 0.02
relaxation = 0.8
charge_scale = 0.07

PLANES = 4
HALO = 6
OWN = HALO
WINDOW = PLANES + 2 * HALO
PAD = 8
CHUNKS = 8
LAG = 3
EARLY = 2
ROOM = 8192
HALVES = 2
MOST = (4, 4, 8)
STEP = NY // CHUNKS
HALF = NY // HALVES
CENTRE = [6.0 + screening * 4.0**level for level in range(4)]
GAIN = [relaxation / centre for centre in CENTRE]
KEEP = 1.0 - relaxation


def sines(n):
    k = np.arange(1, n + 1)
    basis = np.sqrt(2.0 / (n + 1)) * np.sin(np.pi * np.outer(k, k) / (n + 1))
    return basis, 2.0 * np.cos(np.pi * k / (n + 1))


def coarse_basis(depth):
    rows, cols, copies = NY // 8, NX // 8, 8
    sz, ez = sines(depth)
    sy, ey = sines(rows)
    sx, ex = sines(cols)
    left = np.kron(sz, sy)
    into = np.zeros((NX, NX))
    into[::copies, :cols] = sx
    back = np.zeros((NX, NX))
    back[:cols] = np.repeat(sx, copies, axis=1)
    near = (ez[:, None] + ey[None, :]).reshape(-1, 1) + ex[None, :]
    rate = KEEP + GAIN[3] * near
    total = GAIN[3] * sum(rate**n for n in range(COARSE))
    weight = np.zeros((depth * rows, NX))
    weight[:, :cols] = total
    return [np.asarray(part, np.float32) for part in (left, into, back, weight)]


def kernel(
    bands, domains, scale,
    occupations, orbitals, left_in, into_in, back_in, weight_in,
    out,
    occ, left, into, back, weight, held, mixed, out_s, table_s, held_s,
    acc, from_outer, from_inner, fx, va, vb, vc, hv, t0, t1, t2, t3, g,
    share, share_outer, share_inner, shares,
    f1, u1a, u1b, f2, u2a, u2b, f3,
    up_s, up_r, mid_s, mid_r, down_s, down_r, near_s, near_r, far_s, far_r, hv_s, hv_r,
    sum_s, sum_r, share_s, share_r, pass_s, pass_r,
):
    b = lax.axis_index("band")
    d = lax.axis_index("dom")
    half = bands // 2
    lower = b < half
    inner = jnp.where(lower, b + 1, b - 1)
    outer = jnp.where(lower, b - 1, b + 1)
    has_outer = jnp.logical_and(b > 0, b < bands - 1)
    centre = jnp.logical_or(b == half - 1, b == half)
    n1, n2, n3 = 2 * domains, domains, domains // 2

    def remote(src, dst, ss, rs, dev):
        return pltpu.make_async_remote_copy(
            src_ref=src, dst_ref=dst, send_sem=ss, recv_sem=rs,
            device_id=dev, device_id_type=pl.DeviceIdType.MESH,
        )

    lines = STEP * PLANES

    def fetch(c):
        at = (slice(None), pl.ds(c * lines, lines), slice(None))
        return pltpu.make_async_copy(orbitals.at[at], held.at[at], held_s.at[c])

    def result(p):
        r0, rn = blocks(0)[p]
        rows = pl.ds(r0 * PLANES, rn * PLANES)
        return pltpu.make_async_copy(mixed.at[rows], out.at[rows], out_s.at[p])

    tables = [
        pltpu.make_async_copy(src, dst, table_s.at[i])
        for i, (src, dst) in enumerate(
            ((occupations, occ), (left_in, left), (into_in, into), (back_in, back), (weight_in, weight))
        )
    ]
    tables[0].start()
    for c in range(CHUNKS):
        fetch(c).start()
    for table in tables[1:]:
        table.start()
    barrier = pltpu.get_barrier_semaphore()

    def greet(dev):
        pl.semaphore_signal(barrier, inc=1, device_id=dev, device_id_type=pl.DeviceIdType.MESH)

    for i in range(1, domains):
        greet((b, lax.rem(d + i, domains)))
    greet((inner, d))

    @pl.when(has_outer)
    def _():
        greet((outer, d))

    for ref in (fx, va, vb, vc, f1, u1a, u1b, f2, u2a, u2b):
        edge = jnp.zeros((ref.shape[0], PAD, NX), jnp.float32)
        ref[:, 0:PAD, :] = edge
        ref[:, ref.shape[1] - PAD:ref.shape[1], :] = edge

    def clear(ref, p):
        ref[p] = jnp.zeros(ref.shape[1:], jnp.float32)

    for ref in (f1, u1a, u1b, f2, u2a, u2b):
        clear(ref, 0)
        clear(ref, ref.shape[0] - 1)
    clear(vc, OWN - 2)
    clear(vc, OWN + 5)
    for p in (OWN - 2, OWN - 1, OWN + 4, OWN + 5):
        clear(va, p)
    for p in (OWN - 3, OWN - 2, OWN + 5, OWN + 6):
        clear(vb, p)
    for k in range(HALO):
        reach = -(-(HALO - k) // PLANES)

        @pl.when(d < reach)
        def _():
            clear(fx, k)

        @pl.when(d >= domains - reach)
        def _():
            clear(fx, WINDOW - 1 - k)

    def density(c):
        fetch(c).wait()
        first_row = c * lines
        total = None
        for i in range(orbitals.shape[0]):
            value = held[i, first_row:first_row + lines, :].astype(jnp.float32)
            term = (occ[i].astype(jnp.float32) * scale) * (value * value)
            total = term if total is None else total + term
        mixed[first_row:first_row + lines, :] = total
        for p in range(PLANES):
            plane = mixed[pl.ds(first_row + p, STEP, stride=PLANES), :]
            acc[p, c * STEP:(c + 1) * STEP, :] = plane
            va[OWN + p, PAD + c * STEP:PAD + (c + 1) * STEP, :] = plane

    tables[0].wait()
    for c in range(EARLY):
        density(c)
    pl.semaphore_wait(barrier, domains + jnp.where(has_outer, 1, 0))

    def part(ref, c):
        return ref.at[:, pl.ds(c * STEP, STEP), :]

    def slab(c):
        return fx.at[pl.ds(OWN, PLANES), pl.ds(PAD + c * STEP, STEP), :]

    def up(c):
        return remote(part(acc, c), part(from_outer, c), up_s.at[c], up_r.at[c], (inner, d))

    def mid(c):
        return remote(part(acc, c), part(from_inner, c), mid_s.at[c], mid_r.at[c], (inner, d))

    def down(c, dev):
        return remote(slab(c), slab(c), down_s.at[c], down_r.at[c], (dev, d))

    def near_up(c):
        rows = pl.ds(PAD + c * STEP, STEP)
        return remote(
            fx.at[pl.ds(OWN + 2, 2), rows, :], fx.at[pl.ds(OWN - 2, 2), rows, :],
            near_s.at[0, c], near_r.at[0, c], (b, d + 1),
        )

    def near_down(c):
        rows = pl.ds(PAD + c * STEP, STEP)
        return remote(
            fx.at[pl.ds(OWN, 2), rows, :], fx.at[pl.ds(OWN + 4, 2), rows, :],
            near_s.at[1, c], near_r.at[1, c], (b, d - 1),
        )

    even_d = lax.rem(d, 2) == 0
    odd_d = lax.rem(d, 2) == 1
    far = [
        (OWN, OWN - 4, 1, d < domains - 1, d > 0),
        (OWN + 2, OWN + 6, -1, d > 0, d < domains - 1),
        (OWN + 2, OWN - 6, 2, jnp.logical_and(even_d, d < domains - 2), d > 1),
        (OWN, OWN + 8, -2, jnp.logical_and(odd_d, d > 1), d < domains - 2),
    ]

    def far_copy(i, h):
        at, to, offset, _, _ = far[i]
        rows = pl.ds(PAD + h * HALF, HALF)
        return remote(
            fx.at[pl.ds(at, 2), rows, :], fx.at[pl.ds(to, 2), rows, :],
            far_s.at[i, h], far_r.at[i, h], (b, d + offset),
        )

    onward = [
        (OWN - 2, OWN - 6, 1, 2, jnp.logical_and(even_d, d > 1)),
        (OWN + 4, OWN + 8, -1, 3, jnp.logical_and(odd_d, d < domains - 2)),
    ]

    def onward_copy(i, h):
        at, to, offset, slot, _ = onward[i]
        rows = pl.ds(PAD + h * HALF, HALF)
        return remote(
            fx.at[pl.ds(at, 2), rows, :], fx.at[pl.ds(to, 2), rows, :],
            far_s.at[slot + 2, h], far_r.at[slot, h], (b, d + offset),
        )

    def gathered(c, at_centre):
        rows = slice(c * STEP, (c + 1) * STEP)

        @pl.when(has_outer)
        def _():
            up(c).wait_recv()
            acc[:, rows, :] = acc[:, rows, :] + from_outer[:, rows, :]

        (mid(c) if at_centre else up(c)).start()

    def spread(c, at_centre):
        rows = slice(c * STEP, (c + 1) * STEP)
        if at_centre:
            mid(c).wait_recv()
            fx[OWN:OWN + PLANES, PAD + c * STEP:PAD + (c + 1) * STEP, :] = (
                acc[:, rows, :] + from_inner[:, rows, :]
            )
        else:
            down(c, inner).wait_recv()

        @pl.when(has_outer)
        def _():
            down(c, outer).start()

        @pl.when(d < domains - 1)
        def _():
            near_up(c).start()

        @pl.when(d > 0)
        def _():
            near_down(c).start()

        if (c + 1) % (CHUNKS // HALVES) == 0:
            for i in range(4):
                @pl.when(far[i][3])
                def _():
                    far_copy(i, c // (CHUNKS // HALVES)).start()

    def beside(src, p, r0, rn, width):
        c = src[p, PAD + r0:PAD + r0 + rn, :]
        lane = lax.broadcasted_iota(jnp.int32, (rn, NX), 1)
        total = src[p, PAD + r0 - 1:PAD + r0 + rn - 1, :] + src[p, PAD + r0 + 1:PAD + r0 + rn + 1, :]
        total = total + (src[p - 1, PAD + r0:PAD + r0 + rn, :] + src[p + 1, PAD + r0:PAD + r0 + rn, :])
        total = total + jnp.where(lane < width, 0.0, pltpu.roll(c, width, 1))
        total = total + jnp.where(lane >= NX - width, 0.0, pltpu.roll(c, NX - width, 1))
        return c, total

    def rows_of(level):
        return NY >> level

    def blocks(level):
        rn = 48 if rows_of(level) % 48 == 0 else rows_of(level)
        return [(r0, rn) for r0 in range(0, rows_of(level), rn)]

    def loop(lo, count, fn, most=4):
        group = max(n for n in range(1, most + 1) if count % n == 0)

        def step(i, carry):
            for j in range(group):
                fn(lo + i * group + j, j)
            return carry

        lax.fori_loop(0, count // group, step, 0)

    def gain(level, p):
        if level:
            return GAIN[level]
        z = PLANES * d - OWN + p
        inside = jnp.logical_and(z >= 0, z < PLANES * domains)
        return jnp.where(inside, jnp.float32(GAIN[0]), jnp.float32(0.0))

    def first(src, dst, level, lo, count):
        def plane(p, j):
            k = gain(level, p)
            for r0, rn in blocks(level):
                c, total = beside(src, p, r0, rn, 1 << level)
                dst[p, PAD + r0:PAD + r0 + rn, :] = (GAIN[level] * (1.0 + KEEP)) * c + (k * GAIN[level]) * total

        loop(lo, count, plane, MOST[level])

    def sweep(src, source, dst, level, lo, count):
        def plane(p, j):
            k = gain(level, p)
            for r0, rn in blocks(level):
                c, total = beside(src, p, r0, rn, 1 << level)
                f = source[p, PAD + r0:PAD + r0 + rn, :]
                dst[p, PAD + r0:PAD + r0 + rn, :] = KEEP * c + k * (f + total)

        loop(lo, count, plane, MOST[level])

    def residual(v, source, level, p, r0, rn):
        c, total = beside(v, p, r0, rn, 1 << level)
        return source[p, PAD + r0:PAD + r0 + rn, :] + total - CENTRE[level] * c

    spare = (t0, t1, t2, t3)

    def pooled(v, source, level, p, t):
        for r0, rn in blocks(level):
            t[r0:r0 + rn, :] = residual(v, source, level, p, r0, rn) + residual(v, source, level, p + 1, r0, rn)
        n = rows_of(level) // 2
        return t[pl.ds(0, n, stride=2), :] + t[pl.ds(1, n, stride=2), :]

    def window(h):
        return OWN - h, PLANES + 2 * h

    rows1 = NY // 2
    even = lax.broadcasted_iota(jnp.int32, (rows1, NX), 1) % 2 == 0

    def packed(v, source, at, to):
        a = pooled(v, source, 0, at, t0)
        a = a + pltpu.roll(a, NX - 1, 1)
        e = pooled(v, source, 0, to, t1)
        e = e + pltpu.roll(e, 1, 1)
        return 0.5 * jnp.where(even, a, e)

    def restrict_and_send(v, cycle):
        for slot in (1, 2):
            low = (slot - 1) * NY // 2
            pairs = []
            for at, t in ((OWN, t0), (OWN + 2, t1)):
                for r0 in range(low, low + NY // 2, 48):
                    t[r0:r0 + 48, :] = residual(v, fx, 0, at, r0, 48) + residual(v, fx, 0, at + 1, r0, 48)
                n = rows1 // 2
                pairs.append(t[pl.ds(low, n, stride=2), :] + t[pl.ds(low + 1, n, stride=2), :])
            a = pairs[0] + pltpu.roll(pairs[0], NX - 1, 1)
            e = pairs[1] + pltpu.roll(pairs[1], 1, 1)
            g[cycle, d, low // 2:low // 2 + n, :] = 0.5 * jnp.where(even[:n], a, e)
            for i in range(1, chips):
                tell(i, slot).start()
            tell(0, slot).start()

    sibling = d + 1 - 2 * lax.rem(d, 2)
    chips = domains // 2

    def sum_up():
        return remote(share, share_outer, sum_s.at[0], sum_r.at[0], (inner, d))

    def sum_mid():
        return remote(share, share_inner, sum_s.at[1], sum_r.at[1], (inner, d))

    def sum_down(dev):
        return remote(shares.at[d], shares.at[d], sum_s.at[2], sum_r.at[2], (dev, d))

    def block(cycle, origin):
        if cycle == 0:
            return shares.at[origin]
        return g.at[1, origin, pl.ds((cycle - 1) * (rows1 // 2), rows1 // 2), :]

    def tell(i, cycle):
        dev = sibling if i == 0 else lax.rem(d + 2 * i, domains)
        src = block(cycle, d)
        return remote(src, src, share_s.at[cycle, i], share_r.at[cycle, i], (b, dev))

    def origin_of(i, near):
        return sibling if i == 0 else lax.rem(near + (domains - 2 * i), domains)

    def told(i, cycle):
        origin = origin_of(i, d)
        src = block(cycle, origin)
        return remote(src, src, share_s.at[cycle, i], share_r.at[cycle, i], (b, origin))

    def hand_on(i, cycle):
        src = block(cycle, origin_of(i, d))
        return remote(src, src, pass_s.at[cycle, i], pass_r.at[cycle, i], (b, sibling))

    def handed(i, cycle):
        src = block(cycle, origin_of(i, sibling))
        return remote(src, src, pass_s.at[cycle, i], pass_r.at[cycle, i], (b, sibling))

    def make_share():
        first(va, vb, 0, *window(1))
        share[0] = packed(vb, va, OWN, OWN + 2)
        share[1] = packed(vb, va, OWN - 2, OWN + 4)

    def gather_share(at_centre):
        @pl.when(has_outer)
        def _():
            sum_up().wait_recv()
            share[...] = share[...] + share_outer[...]

        (sum_mid() if at_centre else sum_up()).start()

    def spread_share(at_centre):
        if at_centre:
            sum_mid().wait_recv()
            shares[d] = share[...] + share_inner[...]
        else:
            sum_down(inner).wait_recv()

        @pl.when(has_outer)
        def _():
            sum_down(outer).start()

        for i in range(1, chips):
            tell(i, 0).start()
        tell(0, 0).start()

    order = list(range(EARLY)) + [None] + list(range(EARLY, CHUNKS))

    def gather_step(n, at_centre):
        if order[n] is None:
            gather_share(at_centre)
        else:
            gathered(order[n], at_centre)

    def spread_step(n, at_centre):
        if order[n] is None:
            spread_share(at_centre)
        else:
            spread(order[n], at_centre)

    def total_share(e, j):
        below = shares[jnp.maximum(e - 1, 0), 1] * jnp.where(e > 0, 1.0, 0.0)
        above = shares[jnp.minimum(e + 1, domains - 1), 1] * jnp.where(e < domains - 1, 1.0, 0.0)
        a = shares[e, 0] + jnp.where(even, pltpu.roll(below, NX - 1, 1), pltpu.roll(above, 1, 1))
        f1[1 + 2 * e, PAD:PAD + rows1, :] = jnp.where(even, a, pltpu.roll(a, 1, 1))
        f1[2 + 2 * e, PAD:PAD + rows1, :] = jnp.where(even, pltpu.roll(a, NX - 1, 1), a)

    def gathered_shares():
        told(0, 0).wait_recv()
        for i in range(1, chips):
            handed(i, 0).wait_recv()
        loop(0, domains, total_share, 2)

    def v_up():
        return remote(
            vc.at[pl.ds(OWN + 2, 2), pl.ds(PAD, NY), :], hv.at[0], hv_s.at[0], hv_r.at[0], (b, d + 1)
        )

    def v_down():
        return remote(
            vc.at[pl.ds(OWN, 2), pl.ds(PAD, NY), :], hv.at[1], hv_s.at[1], hv_r.at[1], (b, d - 1)
        )

    def gathered_residuals():
        for slot in (1, 2):
            for i in range(1, chips):
                told(i, slot).wait_recv()
                hand_on(i, slot).start()

        @pl.when(d < domains - 1)
        def _():
            v_up().start()

        @pl.when(d > 0)
        def _():
            v_down().start()

        unpack(1, d)
        for i in range(1, chips):
            unpack(1, origin_of(i, d))
        told(0, 1).wait_recv()
        told(0, 2).wait_recv()
        unpack(1, sibling)
        for i in range(1, chips):
            handed(i, 1).wait_recv()
            handed(i, 2).wait_recv()
            unpack(1, origin_of(i, sibling))

    def unpack(cycle, origin):
        a = g[cycle, origin]
        f1[1 + 2 * origin, PAD:PAD + rows1, :] = jnp.where(even, a, pltpu.roll(a, 1, 1))
        f1[2 + 2 * origin, PAD:PAD + rows1, :] = jnp.where(even, pltpu.roll(a, NX - 1, 1), a)

    def widen(a, level):
        width = 1 << level
        lane = lax.broadcasted_iota(jnp.int32, a.shape, 1)
        low = (lane // width) % 2 == 0
        return 0.5 * (a + jnp.where(low, pltpu.roll(a, NX - width, 1), pltpu.roll(a, width, 1)))

    def add_rows(dst, p, value, n):
        for odd in range(2):
            at = (p, pl.ds(PAD + odd, n, stride=2), slice(None))
            dst[at] = dst[at] + value

    def coarse(arrive, near, between):
        arrive()
        first(f1, u1a, 1, 1, n1)

        def down1(q, j):
            f2[1 + q, PAD:PAD + NY // 4, :] = widen(pooled(u1a, f1, 1, 1 + 2 * q, spare[j]), 1)

        loop(0, n2, down1)
        between()
        first(f2, u2a, 2, 1, n2)
        rows3 = NY // 8

        def down2(q, j):
            f3[pl.ds(pl.multiple_of(q * rows3, 8), rows3), :] = widen(pooled(u2a, f2, 2, 1 + 2 * q, spare[j]), 2)

        loop(0, n3, down2)
        dot = functools.partial(
            jnp.dot, precision=lax.Precision.HIGHEST, preferred_element_type=jnp.float32
        )
        modes = dot(left[...], dot(f3[...], into[...])) * weight[...]
        f3[...] = dot(dot(left[...], modes), back[...])

        def back2(q, j):
            value = f3[pl.ds(pl.multiple_of(q * rows3, 8), rows3), :]
            add_rows(u2a, 1 + 2 * q, value, rows3)
            add_rows(u2a, 2 + 2 * q, value, rows3)

        loop(0, n3, back2)
        sweep(u2a, f2, u2b, 2, 1, n2)
        sweep(u2b, f2, u2a, 2, 1, n2)

        def back1(q, j):
            value = u2a[1 + q, PAD:PAD + NY // 4, :]
            add_rows(u1a, 1 + 2 * q, value, NY // 4)
            add_rows(u1a, 2 + 2 * q, value, NY // 4)

        loop(0, n2, back1)
        for extra, src, dst in ((1, u1a, u1b), (0, u1b, u1a)):
            count = min(n1, 2 + 2 * (near + extra))
            start = jnp.clip(2 * d - near - extra, 0, n1 - count)
            sweep(src, f1, dst, 1, start + 1, count)

    def correct(v, planes):
        for p in planes:
            j = (p - OWN) // 2
            z = 2 * d + j

            @pl.when(jnp.logical_and(z >= 0, z < n1))
            def _():
                add_rows(v, p, u1a[z + 1, PAD:PAD + rows1, :], rows1)

    @pl.when(jnp.logical_not(centre))
    def _():
        for n in range(EARLY):
            gather_step(n, False)

    for c in range(EARLY, CHUNKS):
        density(c)
    make_share()

    @pl.when(centre)
    def _():
        for n in range(len(order) + LAG):
            if n < len(order):
                gather_step(n, True)
            if n >= LAG:
                spread_step(n - LAG, True)

    @pl.when(jnp.logical_not(centre))
    def _():
        for n in range(EARLY, len(order)):
            gather_step(n, False)
        for n in range(len(order)):
            spread_step(n, False)

    for i in range(1, chips):
        told(i, 0).wait_recv()
        hand_on(i, 0).start()

    def near_arrived():
        for c in range(CHUNKS):
            @pl.when(d < domains - 1)
            def _():
                near_down(c).wait_recv()

            @pl.when(d > 0)
            def _():
                near_up(c).wait_recv()

        for i in range(2):
            @pl.when(onward[i][4])
            def _():
                for h in range(HALVES):
                    onward_copy(i, h).start()

        for table in tables[1:]:
            table.wait()

    coarse(gathered_shares, 3, near_arrived)
    first(fx, vb, 0, *window(1))
    correct(vb, range(OWN - 1, OWN + 5))
    sweep(vb, fx, va, 0, *window(0))

    for i in range(4):
        @pl.when(far[i][4])
        def _():
            for h in range(HALVES):
                far_copy(i, h).wait_recv()

    first(fx, vb, 0, OWN - 5, 4)
    first(fx, vb, 0, OWN + PLANES + 1, 4)
    correct(vb, [*range(OWN - 5, OWN - 1), *range(OWN + 5, OWN + 9)])
    sweep(vb, fx, va, 0, OWN - 4, 4)
    sweep(vb, fx, va, 0, OWN + 4, 4)
    sweep(va, fx, vb, 0, *window(3))

    sweep(vb, fx, va, 0, *window(2))
    sweep(va, fx, vc, 0, *window(1))
    restrict_and_send(vc, 1)

    coarse(gathered_residuals, 1, lambda: None)

    @pl.when(d < domains - 1)
    def _():
        v_up().wait_send()
        v_down().wait_recv()
        vc[OWN + 4:OWN + 6, PAD:PAD + NY, :] = hv[1]

    @pl.when(d > 0)
    def _():
        v_down().wait_send()
        v_up().wait_recv()
        vc[OWN - 2:OWN, PAD:PAD + NY, :] = hv[0]

    for c in range(CHUNKS):
        @pl.when(centre)
        def _():
            mid(c).wait_send()

        @pl.when(jnp.logical_not(centre))
        def _():
            up(c).wait_send()

    correct(vc, range(OWN - 2, OWN + 6))
    sweep(vc, fx, va, 0, *window(1))
    for k, (r0, rn) in enumerate(blocks(0)):
        for p in range(PLANES):
            c, total = beside(va, OWN + p, r0, rn, 1)
            f = fx[OWN + p, PAD + r0:PAD + r0 + rn, :]
            mixed[pl.ds(r0 * PLANES + p, rn, stride=PLANES), :] = KEEP * c + GAIN[0] * (f + total)
        result(k).start()
    for k in range(len(blocks(0))):
        result(k).wait()

    for c in range(CHUNKS):
        @pl.when(has_outer)
        def _():
            down(c, outer).wait_send()

        @pl.when(d < domains - 1)
        def _():
            near_up(c).wait_send()

        @pl.when(d > 0)
        def _():
            near_down(c).wait_send()

    for i in range(4):
        @pl.when(far[i][3])
        def _():
            for h in range(HALVES):
                far_copy(i, h).wait_send()

    for i in range(2):
        @pl.when(onward[i][4])
        def _():
            for h in range(HALVES):
                onward_copy(i, h).wait_send()

    for cycle in range(3):
        for i in range(chips):
            tell(i, cycle).wait_send()
        for i in range(1, chips):
            hand_on(i, cycle).wait_send()

    @pl.when(centre)
    def _():
        sum_mid().wait_send()

    @pl.when(jnp.logical_not(centre))
    def _():
        sum_up().wait_send()

    @pl.when(has_outer)
    def _():
        sum_down(outer).wait_send()


def potential_of(orbitals, occupations, bands, domains):
    n1, n2, n3 = 2 * domains, domains, domains // 2
    tables = coarse_basis(n3)
    f32 = jnp.float32
    count = orbitals.shape[0]
    pair = pltpu.VMEM((2, NY // 2, NX), f32)
    slab = pltpu.VMEM((PLANES, NY, NX), f32)
    fine = pltpu.VMEM((WINDOW, NY + 2 * PAD, NX), f32)
    level1 = pltpu.VMEM((n1 + 2, NY // 2 + 2 * PAD, NX), f32)
    level2 = pltpu.VMEM((n2 + 2, NY // 4 + 2 * PAD, NX), f32)
    chunk_sems = pltpu.SemaphoreType.DMA((CHUNKS,))
    near_sems = pltpu.SemaphoreType.DMA((2, CHUNKS))
    sum_sems = pltpu.SemaphoreType.DMA((3,))
    chip_sems = pltpu.SemaphoreType.DMA((3, domains // 2))
    return pl.pallas_call(
        functools.partial(kernel, bands, domains, 0.5 * charge_scale / (count * bands)),
        out_shape=jax.ShapeDtypeStruct((ROOM, NX), f32),
        in_specs=[pl.BlockSpec(memory_space=pl.ANY)] * 6,
        out_specs=pl.BlockSpec(memory_space=pl.ANY),
        scratch_shapes=[
            pltpu.SMEM(occupations.shape, jnp.int32),
            *[pltpu.VMEM(table.shape, f32) for table in tables],
            pltpu.VMEM(orbitals.shape, orbitals.dtype),
            pltpu.VMEM((NY * PLANES, NX), f32),
            pltpu.SemaphoreType.DMA((8,)), pltpu.SemaphoreType.DMA((5,)), chunk_sems,
            slab, slab, slab, fine, fine, fine, fine,
            pltpu.VMEM((2, 2, NY, NX), f32),
            *[pltpu.VMEM((NY, NX), f32)] * 4,
            pltpu.VMEM((2, domains, NY // 2, NX), f32),
            pair, pair, pair, pltpu.VMEM((domains, 2, NY // 2, NX), f32),
            level1, level1, level1, level2, level2, level2,
            pltpu.VMEM((n3 * (NY // 8), NX), f32),
            chunk_sems, chunk_sems, chunk_sems, chunk_sems, chunk_sems, chunk_sems,
            near_sems, near_sems,
            pltpu.SemaphoreType.DMA((6, HALVES)), pltpu.SemaphoreType.DMA((4, HALVES)),
            pltpu.SemaphoreType.DMA((2,)), pltpu.SemaphoreType.DMA((2,)),
            sum_sems, sum_sems, chip_sems, chip_sems, chip_sems, chip_sems,
        ],
        compiler_params=pltpu.CompilerParams(
            collective_id=0, has_side_effects=True, vmem_limit_bytes=62_500_000
        ),
    )(occupations, orbitals, *[jnp.asarray(table) for table in tables])


def apply(mixed_in, orbitals, potential, applied, mixed, held, in_s, keep_s, held_s):
    rows = STEP * PLANES

    def part(c):
        return (slice(None), pl.ds(c * rows, rows), slice(None))

    def fetch(c):
        at = pl.ds(c * rows, rows)
        return pltpu.make_async_copy(mixed_in.at[at], mixed.at[at], in_s.at[c])

    def keep(c):
        at = pl.ds(c * rows, rows)
        return pltpu.make_async_copy(mixed.at[at], potential.at[at], keep_s.at[c])

    def store(c):
        return pltpu.make_async_copy(held.at[part(c)], applied.at[part(c)], held_s.at[c])

    for c in range(CHUNKS):
        fetch(c).start()
    for c in range(CHUNKS):
        fetch(c).wait()
        keep(c).start()
        value = mixed[c * rows:(c + 1) * rows, :]
        for i in range(orbitals.shape[0]):
            psi = orbitals[i, c * rows:(c + 1) * rows, :].astype(jnp.float32)
            held[i, c * rows:(c + 1) * rows, :] = (value * psi).astype(held.dtype)
        store(c).start()
    for c in range(CHUNKS):
        keep(c).wait()
        store(c).wait()


def cells_of(orbitals):
    count = orbitals.shape[0]
    cells = orbitals.reshape(count, PLANES, NY, NX).transpose(0, 2, 1, 3)
    return cells.reshape(count, NY * PLANES, NX)


def applied_of(mixed, cells):
    sems = pltpu.SemaphoreType.DMA((CHUNKS,))
    anywhere = pl.BlockSpec(memory_space=pl.ANY)
    count = cells.shape[0]
    potential, applied = pl.pallas_call(
        apply,
        out_shape=(
            jax.ShapeDtypeStruct((NY * PLANES, NX), jnp.float32),
            jax.ShapeDtypeStruct(cells.shape, cells.dtype),
        ),
        in_specs=[anywhere, pl.BlockSpec(memory_space=pltpu.VMEM)],
        out_specs=(anywhere, anywhere),
        scratch_shapes=[
            pltpu.VMEM((NY * PLANES, NX), jnp.float32),
            pltpu.VMEM(cells.shape, cells.dtype),
            sems, sems, sems,
        ],
        compiler_params=pltpu.CompilerParams(vmem_limit_bytes=54_200_000),
    )(mixed, cells)
    applied = applied.reshape(count, NY, PLANES, NX).transpose(0, 2, 1, 3)
    potential = potential.reshape(NY, PLANES, NX).transpose(1, 0, 2)
    return potential.reshape(PLANES, NY * NX), applied.reshape(count, PLANES, NY * NX)


def body(bands, domains, orbitals, occupations):
    cells = cells_of(orbitals)
    return applied_of(potential_of(cells, occupations, bands, domains), cells)


def solution(mesh):
    return jax.shard_map(
        functools.partial(body, mesh.shape["band"], mesh.shape["dom"]),
        mesh=mesh,
        in_specs=(P("band", "dom", None), P("band")),
        out_specs=(P("dom", None), P("band", "dom", None)),
        check_vma=False,
    )
```
